512 devices in a mesh: ctx: 32 (over y, z_lo, core), fsdp: 16 (over x, z_hi).
Axes of the slice: x: 4, y: 4, z: 16 (z_hi: 4, z_lo: 4; z = z_hi * 4 + z_lo), core: 2. Of those that a mesh axis runs over, the one named last changes fastest.
Arguments:
- query: bfloat16 [16384, 8192], P('ctx', 'fsdp'), may hold values from -6 to 6
- key_in: bfloat16 [16384, 8192], P('ctx', 'fsdp'), may hold values from -6 to 6
- value_in: bfloat16 [16384, 8192], P('ctx', 'fsdp'), may hold values from -6 to 6
- cotangent: bfloat16 [16384, 8192], P('ctx', 'fsdp'), may hold values from -6 to 6
- filter_weight: float32 [128, 512], P('fsdp', 'ctx'), may hold values from -0.5 to 0.5
- log_rate: float32 [512], P('ctx'), may hold values from -6 to -3
Outputs:
- output: bfloat16 [16384, 8192], P('ctx', 'fsdp')
- grad_query: bfloat16 [16384, 8192], P('ctx', 'fsdp')
- grad_key: bfloat16 [16384, 8192], P('ctx', 'fsdp')
- grad_value: bfloat16 [16384, 8192], P('ctx', 'fsdp')
- grad_filter: float32 [128, 512], P('fsdp', 'ctx')
- grad_log_rate: float32 [512], P('ctx')
The draws below stay inside these ranges and needn't reach their ends.
All inputs are finite; a program needn't handle non-finite values.
Results may differ from the reference program's by a relative error of at most 0.0057.
Values may be sent and summed in bfloat16 or wider, within the bound.
No kernel may reach another device: no remote copies, remote signals or barrier semaphores. Data moves between devices by JAX's collectives and lax.ppermute only.
A program may use at most 64 MiB of HBM per device.

```python
import math
import jax
import jax.numpy as jnp
from jax import lax

C = 8192
FILT = 128
GROUP = 16
TOKENS = 16384
GROUPS = 512


def steps_of(stream_key, shape, shards, low, largest):
    factor_of = 1.0
    for dim, parts in shards:
        steps = jax.random.uniform(jax.random.fold_in(jax.random.fold_in(stream_key, 6), dim), (parts,), jnp.float32, low / len(shards), largest / len(shards))
        factor_of = factor_of * jnp.repeat(jnp.exp(steps), shape[dim] // parts).reshape((-1,) + (1,) * (len(shape) - 1 - dim))
    return factor_of


def normal_values(own_key, dims, width, reach, shards=(), held_as=jnp.bfloat16):
    level = steps_of(own_key, dims, shards, -0.22, 0.18) if shards else 1.0
    entries = jax.random.normal(own_key, dims, jnp.float32) * width * level
    return jnp.minimum(jnp.maximum(entries, -reach), reach).astype(held_as)


def setup_inputs(seed: int = 0) -> dict:
    streams_of = jax.random.split(jax.random.key(seed), 7)
    query = normal_values(streams_of[0], (TOKENS, C), 1.0, 6.0, ((0, 32), (1, 16)))
    key_in = normal_values(streams_of[1], (TOKENS, C), 1.0, 6.0, ((0, 32), (1, 16)))
    value_in = normal_values(streams_of[2], (TOKENS, C), 1.0, 6.0, ((0, 32), (1, 16)))
    cotangent = normal_values(streams_of[3], (TOKENS, C), 1.0, 6.0, ((0, 32), (1, 16)))
    filter_weight = normal_values(streams_of[4], (FILT, GROUPS), FILT ** -0.5, 0.5, ((0, 16), (1, 32)), jnp.float32)
    log_rate = jnp.clip(-6.0 + 3.0 * jax.random.uniform(streams_of[5], (GROUPS,), jnp.float32) ** steps_of(streams_of[5], (GROUPS,), ((0, 32),), -0.2, 0.2), -6.0, -3.0)
    return {"query": query, "key_in": key_in, "value_in": value_in, "cotangent": cotangent, "filter_weight": filter_weight, "log_rate": log_rate}


def reference(query, key_in, value_in, cotangent, filter_weight, log_rate):
    tap_index = jnp.arange(FILT, dtype=jnp.float32)
    decay_rates = jnp.exp(log_rate)
    decays = jnp.exp(-decay_rates[None, :] * tap_index[:, None])
    filters = (filter_weight * decays).astype(jnp.bfloat16)
    block_width = min(C, 1024)
    block_count = C // block_width
    fft_length = 2 * TOKENS

    def to_blocks(array_in):
        return array_in.reshape(TOKENS, block_count, block_width).transpose(1, 0, 2)

    def from_blocks(array_in):
        return array_in.transpose(1, 0, 2).reshape(TOKENS, C)

    def one_block(pieces):
        query_part, key_part, value_part, cot_part, filter_part = pieces
        channel_filters = jnp.repeat(filter_part.astype(jnp.float32), GROUP, axis=1)
        products = (key_part.astype(jnp.float32) * value_part.astype(jnp.float32)).astype(jnp.bfloat16)
        filter_freq = jnp.fft.rfft(channel_filters, n=fft_length, axis=0)
        product_freq = jnp.fft.rfft(products.astype(jnp.float32), n=fft_length, axis=0)
        mixed_rows = jnp.fft.irfft(product_freq * filter_freq, n=fft_length, axis=0)[:TOKENS]
        query_wide = query_part.astype(jnp.float32)
        cot_wide = cot_part.astype(jnp.float32)
        output_part = (query_wide * mixed_rows).astype(jnp.bfloat16)
        grad_mixed = (cot_wide * query_wide).astype(jnp.bfloat16)
        grad_query_part = (cot_wide * mixed_rows).astype(jnp.bfloat16)
        grad_freq = jnp.fft.rfft(grad_mixed.astype(jnp.float32), n=fft_length, axis=0)
        grad_products = jnp.fft.irfft(grad_freq * jnp.conj(filter_freq), n=fft_length, axis=0)[:TOKENS]
        grad_key_part = (grad_products * value_part.astype(jnp.float32)).astype(jnp.bfloat16)
        grad_value_part = (grad_products * key_part.astype(jnp.float32)).astype(jnp.bfloat16)
        cross_freq = grad_freq * jnp.conj(product_freq)
        cross_freq = cross_freq.reshape(cross_freq.shape[0], block_width // GROUP, GROUP).sum(axis=2)
        filter_part_sums = jnp.fft.irfft(cross_freq, n=fft_length, axis=0)[:FILT]
        return (output_part, grad_query_part, grad_key_part, grad_value_part, filter_part_sums)
    filter_blocks = filters.reshape(FILT, block_count, block_width // GROUP).transpose(1, 0, 2)
    results = lax.map(one_block, (to_blocks(query), to_blocks(key_in), to_blocks(value_in), to_blocks(cotangent), filter_blocks))
    filter_sums = results[4].transpose(1, 0, 2).reshape(FILT, C // GROUP)
    grad_scale = 1.0 / math.sqrt(TOKENS * GROUP)
    grad_filter = filter_sums * decays * grad_scale
    grad_log_rate = lax.optimization_barrier(jnp.sum(filter_sums * filter_weight * decays * (-tap_index[:, None] * decay_rates[None, :]), axis=0)) * grad_scale
    return (from_blocks(results[0]), from_blocks(results[1]), from_blocks(results[2]), from_blocks(results[3]), grad_filter, grad_log_rate)
```

```python
import math

import jax
import jax.numpy as jnp
from jax import lax
from jax.experimental import pallas as pl
from jax.experimental.pallas import tpu as pltpu
from jax.sharding import PartitionSpec as P

FILT = 128
GROUP = 16
LANES = 128
F32 = jnp.float32
BF16 = jnp.bfloat16
VMEM_BYTES = 48 * 1024 * 1024
NT = (((1,), (1,)), ((), ()))


def iota(shape, dim):
    return lax.broadcasted_iota(jnp.int32, shape, dim)


def rounded_product(a, b):
    return (a.astype(F32) * b.astype(F32)).astype(BF16)


def edges_kernel(key_ref, value_ref, query_ref, cot_ref, weight_ref, rate_ref, tail_ref, head_ref, taps_ref):
    tail_ref[...] = rounded_product(key_ref[...], value_ref[...])
    head_ref[...] = rounded_product(cot_ref[...], query_ref[...])
    tap_count, group_count = weight_ref.shape
    first_tap = lax.axis_index("fsdp") * tap_count
    taps = (first_tap + iota((tap_count, group_count), 0)).astype(F32)
    decayed = weight_ref[...] * jnp.exp(-jnp.exp(rate_ref[...]) * taps)
    high = decayed.astype(BF16).astype(F32)
    taps_ref[...] = jnp.zeros_like(taps_ref)
    taps_ref[:, :group_count] = high
    taps_ref[:, group_count : 2 * group_count] = decayed - high


def sums_kernel(key_ref, value_ref, query_ref, cot_ref, next_ref, sums_ref):
    rows = key_ref.shape[0]
    blocks = rows // FILT
    products = rounded_product(key_ref[...], value_ref[...])
    grads = jnp.concatenate([rounded_product(cot_ref[...], query_ref[...]), next_ref[...]], axis=0)
    left = jnp.concatenate([products[b * FILT : (b + 1) * FILT] for b in range(blocks)], axis=1)
    right = jnp.concatenate([grads[b * FILT : (b + 2) * FILT] for b in range(blocks)], axis=1)
    groups = LANES // GROUP
    lane_group = (iota(left.shape, 1) % LANES) // GROUP
    zero = jnp.zeros_like(left)
    stacked = jnp.concatenate([jnp.where(lane_group == g, left, zero) for g in range(groups)], axis=0)
    outer = lax.dot_general(stacked, right, NT, preferred_element_type=F32)
    later = iota((FILT, FILT), 1) >= iota((FILT, FILT), 0)
    rolled = jnp.zeros((groups * 8, LANES), F32)
    merged = [
        jnp.where(later, outer[g * FILT : (g + 1) * FILT, :FILT], outer[g * FILT : (g + 1) * FILT, FILT:])
        for g in range(groups)
    ]
    for i in range(FILT // 8):
        part = jnp.concatenate([m[8 * i : 8 * i + 8] for m in merged], axis=0)
        rolled = rolled + (pltpu.roll(part, FILT - 8 * i, axis=1) if i else part)
    row = iota(rolled.shape, 0) % 8
    for step in (1, 2, 4):
        rolled = jnp.where((row & step) != 0, pltpu.roll(rolled, FILT - step, axis=1), rolled)
    sums_ref[...] = rolled.reshape(groups, 8, LANES).sum(axis=1)


def message_kernel(sums_ref, taps_ref, out_ref):
    half = sums_ref.shape[0] // 2
    taps = taps_ref[...]
    halves = [
        jnp.concatenate([sums_ref[h * half : (h + 1) * half], taps], axis=0).astype(BF16) for h in range(2)
    ]
    for peer in range(out_ref.shape[0]):
        out_ref[peer] = halves[peer % 2]


def reduce_kernel(recv_ref, filt_ref, flipped_ref, home_ref):
    peers, rows, _ = recv_ref.shape
    half = GROUP
    total = jnp.zeros((half, LANES), F32)
    pieces = ([], [])
    for peer in range(peers):
        message = recv_ref[peer].astype(F32)
        total = total + message[:half]
        pieces[peer % 2].append(message[half:])
    eye = (iota((2 * half, LANES), 0) == iota((2 * half, LANES), 1)).astype(F32)
    turned = [
        lax.dot_general(
            eye.astype(BF16), jnp.concatenate(p, axis=0).astype(BF16), NT, preferred_element_type=F32
        )
        for p in pieces
    ]
    high = jnp.concatenate([t[:half] for t in turned], axis=0)
    flip = ((iota((FILT, FILT), 0) + iota((FILT, FILT), 1)) % FILT == 0).astype(BF16)
    filt_ref[...] = high
    flipped_ref[...] = jnp.dot(high.astype(BF16), flip, preferred_element_type=F32)
    own = lax.axis_index("ctx")
    decayed = [t[:half] + t[half:] for t in turned]
    own_decayed = jnp.where(own % 2 == 0, decayed[0], decayed[1])
    lane = iota((half, LANES), 1)
    rate = jnp.sum(own_decayed * total * lane.astype(F32), axis=1, keepdims=True)
    tap_count = 8
    moved = pltpu.roll(total, (FILT - tap_count * (own // 2)) % FILT, axis=1)
    home_ref[...] = jnp.where(lane < tap_count, moved, rate)


def circulants(rows):
    return jnp.concatenate(
        [
            pltpu.roll(jnp.broadcast_to(rows[g : g + 1], (FILT, FILT)), 0, axis=1, stride=1, stride_axis=0)
            for g in range(rows.shape[0])
        ],
        axis=0,
    )


def banded_pair(rows, first, second):
    whole = circulants(rows)
    zero = jnp.zeros_like(whole)
    return jnp.concatenate([jnp.where(first, whole, zero), jnp.where(second, whole, zero)], axis=1).astype(BF16)


def apply_filters(band, padded, blocks):
    right = jnp.concatenate([padded[b * FILT : (b + 2) * FILT] for b in range(blocks)], axis=1)
    wide = jnp.dot(band, right, preferred_element_type=F32)
    lane_group = iota((FILT, LANES), 1) // GROUP
    out = []
    for b in range(blocks):
        kept = wide[:FILT, b * LANES : (b + 1) * LANES]
        for g in range(1, LANES // GROUP):
            kept = jnp.where(
                lane_group == g, wide[g * FILT : (g + 1) * FILT, b * LANES : (b + 1) * LANES], kept
            )
        out.append(kept)
    return out


def outputs_kernel(
    key_ref, value_ref, query_ref, cot_ref, before_ref, after_ref, filt_ref, flipped_ref,
    output_ref, grad_query_ref, grad_key_ref, grad_value_ref,
):
    blocks = key_ref.shape[0] // FILT
    groups = LANES // GROUP
    shape = (groups * FILT, FILT)
    row, col = iota(shape, 0) % FILT, iota(shape, 1)
    above, lower = row < col, row >= col
    key, value = key_ref[...].astype(F32), value_ref[...].astype(F32)
    query, cot = query_ref[...].astype(F32), cot_ref[...].astype(F32)
    products = jnp.concatenate([before_ref[...], (key * value).astype(BF16)], axis=0)
    forward = banded_pair(flipped_ref[...], above, lower)
    for b, mixed in enumerate(apply_filters(forward, products, blocks)):
        rows = slice(b * FILT, (b + 1) * FILT)
        output_ref[rows] = (query[rows] * mixed).astype(BF16)
        grad_query_ref[rows] = (cot[rows] * mixed).astype(BF16)
    grads = jnp.concatenate([(cot * query).astype(BF16), after_ref[...]], axis=0)
    backward = banded_pair(filt_ref[...], row <= col, row > col)
    for b, back in enumerate(apply_filters(backward, grads, blocks)):
        rows = slice(b * FILT, (b + 1) * FILT)
        grad_key_ref[rows] = (back * value[rows]).astype(BF16)
        grad_value_ref[rows] = (back * key[rows]).astype(BF16)


def finish_kernel(home_ref, rate_ref, grad_filter_ref, grad_rate_ref, *, scale):
    tap_count, group_count = grad_filter_ref.shape
    turned = home_ref[...].T
    first_tap = lax.axis_index("fsdp") * tap_count
    taps = (first_tap + iota((tap_count, group_count), 0)).astype(F32)
    rates = jnp.exp(rate_ref[...])
    grad_filter_ref[...] = turned[:tap_count, :group_count] * jnp.exp(-rates * taps) * scale
    grad_rate_ref[...] = turned[tap_count : tap_count + 1, :group_count] * (-rates) * scale


def params():
    return pltpu.CompilerParams(vmem_limit_bytes=VMEM_BYTES)


def swap_axes(value):
    ctx, fsdp = lax.axis_size("ctx"), lax.axis_size("fsdp")
    pairs = [(c * fsdp + f, (2 * f + c % 2) * fsdp + c // 2) for c in range(ctx) for f in range(fsdp)]
    return lax.ppermute(value, ("ctx", "fsdp"), pairs)


def passed_along(value, by):
    peers = lax.axis_size("ctx")
    pairs = [(i, i + by) for i in range(peers) if 0 <= i + by < peers]
    return lax.ppermute(value, "ctx", pairs)


def per_device(query, key_in, value_in, cotangent, filter_weight, log_rate):
    tokens, channels = query.shape
    peers = lax.axis_size("ctx")
    groups = channels // GROUP
    scale = 1.0 / math.sqrt(tokens * peers * GROUP)
    rate_row = log_rate.reshape(1, -1)
    sds = jax.ShapeDtypeStruct
    last = tokens // FILT - 1
    tap_count, tap_groups = filter_weight.shape

    tail_spec = pl.BlockSpec((FILT, channels), lambda i: (last, 0))
    head_spec = pl.BlockSpec((FILT, channels), lambda i: (0, 0))
    tail, head, taps = pl.pallas_call(
        edges_kernel,
        grid=(1,),
        in_specs=[
            tail_spec, tail_spec, head_spec, head_spec,
            pl.BlockSpec(filter_weight.shape, lambda i: (0, 0)),
            pl.BlockSpec(rate_row.shape, lambda i: (0, 0)),
        ],
        out_specs=[head_spec, head_spec, pl.BlockSpec((tap_count, LANES), lambda i: (0, 0))],
        out_shape=[
            sds((FILT, channels), BF16), sds((FILT, channels), BF16), sds((tap_count, LANES), F32),
        ],
        compiler_params=params(),
    )(key_in, value_in, query, cotangent, filter_weight, rate_row)
    after = passed_along(head, -1)
    taps_here = swap_axes(taps)
    before = passed_along(tail, 1)

    tile = pl.BlockSpec((tokens, LANES), lambda i: (0, i))
    halo = pl.BlockSpec((FILT, LANES), lambda i: (0, i))
    group_rows = pl.BlockSpec((LANES // GROUP, LANES), lambda i: (i, 0))
    sums = pl.pallas_call(
        sums_kernel,
        grid=(channels // LANES,),
        in_specs=[tile, tile, tile, tile, halo],
        out_specs=group_rows,
        out_shape=sds((groups, LANES), F32),
        compiler_params=params(),
    )(key_in, value_in, query, cotangent, after)
    message = pl.pallas_call(
        message_kernel,
        out_shape=sds((peers, groups // 2 + tap_count, LANES), BF16),
        compiler_params=params(),
    )(sums, taps_here)
    received = lax.all_to_all(message, "ctx", 0, 0, tiled=True)
    filt, flipped, home = pl.pallas_call(
        reduce_kernel,
        out_shape=[sds((groups, LANES), F32), sds((groups, LANES), F32), sds((groups // 2, LANES), F32)],
        compiler_params=params(),
    )(received)
    home = swap_axes(home)
    output, grad_query, grad_key, grad_value = pl.pallas_call(
        outputs_kernel,
        grid=(channels // LANES,),
        in_specs=[tile, tile, tile, tile, halo, halo, group_rows, group_rows],
        out_specs=[tile] * 4,
        out_shape=[sds((tokens, channels), BF16)] * 4,
        compiler_params=params(),
    )(key_in, value_in, query, cotangent, before, after, filt, flipped)
    grad_filter, grad_rate = pl.pallas_call(
        lambda *refs: finish_kernel(*refs, scale=scale),
        out_shape=[sds(filter_weight.shape, F32), sds(rate_row.shape, F32)],
        compiler_params=params(),
    )(home, rate_row)
    return (output, grad_query, grad_key, grad_value, grad_filter, grad_rate.reshape(log_rate.shape))


def solution(mesh):
    specs = (P("ctx", "fsdp"),) * 4 + (P("fsdp", "ctx"), P("ctx"))
    return jax.shard_map(per_device, mesh=mesh, in_specs=specs, out_specs=specs, check_vma=False)
```

```python
import math

import jax
import jax.numpy as jnp
from jax import lax
from jax.experimental import pallas as pl
from jax.experimental.pallas import tpu as pltpu
from jax.sharding import PartitionSpec as P

FILT = 128
GROUP = 16
LANES = 128
F32 = jnp.float32
BF16 = jnp.bfloat16
MIB = 1024 * 1024
NT = (((1,), (1,)), ((), ()))


def iota(shape, dim):
    return lax.broadcasted_iota(jnp.int32, shape, dim)


def rounded_product(a, b):
    return (a.astype(F32) * b.astype(F32)).astype(BF16)


def front_kernel(key, value, query, cot, weight, rate, tail_ref, head_ref, taps_ref, *scratch):
    refs, sems = scratch[:-1], scratch[-1]
    tail = pl.ds(key.shape[0] - FILT, FILT)
    head = pl.ds(0, FILT)
    sources = [weight, rate, cot.at[head], query.at[head], key.at[tail], value.at[tail]]
    copies = [pltpu.make_async_copy(s, d, sems.at[i]) for i, (s, d) in enumerate(zip(sources, refs))]
    for copy in copies:
        copy.start()
    weight_ref, rate_ref, cot_ref, query_ref, key_ref, value_ref = refs
    copies[0].wait()
    copies[1].wait()
    tap_count, group_count = weight.shape
    taps = (lax.axis_index("fsdp") * tap_count + iota((tap_count, group_count), 0)).astype(F32)
    decayed = weight_ref[...] * jnp.exp(-jnp.exp(rate_ref[...]) * taps)
    high = decayed.astype(BF16).astype(F32)
    taps_ref[...] = jnp.zeros_like(taps_ref)
    taps_ref[:, :group_count] = high
    taps_ref[:, group_count : 2 * group_count] = decayed - high
    copies[2].wait()
    copies[3].wait()
    head_ref[...] = rounded_product(cot_ref[...], query_ref[...])
    copies[4].wait()
    copies[5].wait()
    tail_ref[...] = rounded_product(key_ref[...], value_ref[...])


def outer_products(left, right):
    groups = LANES // GROUP
    lane_group = (iota(left.shape, 1) % LANES) // GROUP
    zero = jnp.zeros_like(left)
    stacked = jnp.concatenate([jnp.where(lane_group == g, left, zero) for g in range(groups)], axis=0)
    outer = lax.dot_general(stacked, right, NT, preferred_element_type=F32)
    return [outer[g * FILT : (g + 1) * FILT] for g in range(groups)]


def diagonal_sums(squares):
    rolled = jnp.zeros((len(squares) * 8, LANES), F32)
    for i in range(FILT // 8):
        part = jnp.concatenate([m[8 * i : 8 * i + 8] for m in squares], axis=0)
        rolled = rolled + (pltpu.roll(part, FILT - 8 * i, axis=1) if i else part)
    row = iota(rolled.shape, 0) % 8
    for step in (1, 2, 4):
        rolled = jnp.where((row & step) != 0, pltpu.roll(rolled, FILT - step, axis=1), rolled)
    return rolled.reshape(len(squares), 8, LANES).sum(axis=1)


def same_block():
    return iota((FILT, FILT), 1) >= iota((FILT, FILT), 0)


def sums_kernel(key_ref, value_ref, query_ref, cot_ref, sums_ref):
    blocks = key_ref.shape[0] // FILT
    same = same_block()
    groups = LANES // GROUP
    for tile in range(key_ref.shape[1] // LANES):
        lanes = slice(tile * LANES, (tile + 1) * LANES)
        products = rounded_product(key_ref[:, lanes], value_ref[:, lanes])
        grads = rounded_product(cot_ref[:, lanes], query_ref[:, lanes])
        grads = jnp.concatenate([grads, jnp.zeros((FILT, LANES), BF16)], axis=0)
        left = jnp.concatenate([products[b * FILT : (b + 1) * FILT] for b in range(blocks)], axis=1)
        right = jnp.concatenate([grads[b * FILT : (b + 2) * FILT] for b in range(blocks)], axis=1)
        sums_ref[tile * groups : (tile + 1) * groups] = diagonal_sums(
            [jnp.where(same, outer[:, :FILT], outer[:, FILT:]) for outer in outer_products(left, right)]
        )


def whole_sums_kernel(sums_ref, tail_ref, after_ref, out_ref):
    same = same_block()
    groups = LANES // GROUP
    for tile in range(tail_ref.shape[1] // LANES):
        lanes = slice(tile * LANES, (tile + 1) * LANES)
        rows = slice(tile * groups, (tile + 1) * groups)
        outers = outer_products(tail_ref[:, lanes], after_ref[:, lanes])
        crossing = diagonal_sums([jnp.where(same, jnp.zeros_like(outer), outer) for outer in outers])
        out_ref[rows] = sums_ref[rows] + crossing


def message_kernel(sums_ref, taps_ref, out_ref):
    half = sums_ref.shape[0] // 2
    taps = taps_ref[...]
    halves = [
        jnp.concatenate([sums_ref[h * half : (h + 1) * half], taps], axis=0).astype(BF16) for h in range(2)
    ]
    for peer in range(out_ref.shape[0]):
        out_ref[peer] = halves[peer % 2]


LANDING = ((0, 2, 3, 1), (0, 1, 2, 3), (0, 1, 2, 3), (2, 0, 1, 3))
SIDE = 4


def landing(ctx, fsdp):
    column, half = ctx // 2, ctx % 2
    x, hi = fsdp // SIDE, fsdp % SIDE
    place = (x + 2) % SIDE * SIDE + LANDING[column % SIDE][hi]
    return place * 2 + half, column


def by_column(column, values):
    out = values[1]
    for q in (0, 3):
        out = jnp.where(column % SIDE == q, values[q], out)
    return out


def landed_piece(ctx, column):
    low = ctx // 2 % SIDE
    hi = jnp.int32(0)
    for z in range(SIDE):
        hi = jnp.where(low == z, by_column(column, [jnp.int32(LANDING[q].index(z)) for q in range(SIDE)]), hi)
    return (ctx // 8 + 2) % SIDE * SIDE + hi


def reduce_kernel(recv_ref, filt_ref, flipped_ref, home_ref):
    peers = recv_ref.shape[0]
    half = GROUP
    own, column = lax.axis_index("ctx"), lax.axis_index("fsdp")
    total = jnp.zeros((half, LANES), F32)
    landed = []
    for peer in range(peers):
        message = recv_ref[peer].astype(F32)
        total = total + message[:half]
        landed.append(message[half:])
    eye = (iota((2 * half, LANES), 0) == iota((2 * half, LANES), 1)).astype(BF16)
    turned = []
    for h in range(2):
        pieces = []
        for piece in range(peers // 2):
            x, hi = piece // SIDE, piece % SIDE
            places = [(x + 2) % SIDE * SIDE + LANDING[q][hi] for q in range(SIDE)]
            pieces.append(by_column(column, [landed[2 * place + h] for place in places]))
        pieces = jnp.concatenate(pieces, axis=0).astype(BF16)
        turned.append(lax.dot_general(eye, pieces, NT, preferred_element_type=F32))
    high = jnp.concatenate([t[:half] for t in turned], axis=0)
    flip = ((iota((FILT, FILT), 0) + iota((FILT, FILT), 1)) % FILT == 0).astype(BF16)
    filt_ref[...] = high
    flipped_ref[...] = jnp.dot(high.astype(BF16), flip, preferred_element_type=F32)
    decayed = [t[:half] + t[half:] for t in turned]
    own_decayed = jnp.where(own % 2 == 0, decayed[0], decayed[1])
    lane = iota((half, LANES), 1)
    rate = jnp.sum(own_decayed * total * lane.astype(F32), axis=1, keepdims=True)
    tap_count = FILT * 2 // peers
    moved = pltpu.roll(total, (FILT - tap_count * landed_piece(own, column)) % FILT, axis=1)
    home_ref[...] = jnp.where(lane < tap_count, moved, rate)


def circulants(rows):
    return jnp.concatenate(
        [
            pltpu.roll(jnp.broadcast_to(rows[g : g + 1], (FILT, FILT)), 0, axis=1, stride=1, stride_axis=0)
            for g in range(rows.shape[0])
        ],
        axis=0,
    )


def banded_pair(rows, first, second):
    whole = circulants(rows)
    zero = jnp.zeros_like(whole)
    return jnp.concatenate([jnp.where(first, whole, zero), jnp.where(second, whole, zero)], axis=1).astype(BF16)


def apply_filters(band, padded, blocks):
    right = jnp.concatenate([padded[b * FILT : (b + 2) * FILT] for b in range(blocks)], axis=1)
    wide = jnp.dot(band, right, preferred_element_type=F32)
    lane_group = iota((FILT, LANES), 1) // GROUP
    out = []
    for b in range(blocks):
        kept = wide[:FILT, b * LANES : (b + 1) * LANES]
        for g in range(1, LANES // GROUP):
            kept = jnp.where(
                lane_group == g, wide[g * FILT : (g + 1) * FILT, b * LANES : (b + 1) * LANES], kept
            )
        out.append(kept)
    return out


def outputs_kernel(
    key_ref, value_ref, query_ref, cot_ref, before_ref, after_ref, filt_ref, flipped_ref,
    output_ref, grad_query_ref, grad_key_ref, grad_value_ref,
):
    blocks = key_ref.shape[0] // FILT
    groups = LANES // GROUP
    shape = (groups * FILT, FILT)
    row, col = iota(shape, 0) % FILT, iota(shape, 1)
    above, lower = row < col, row >= col
    key, value = key_ref[...].astype(F32), value_ref[...].astype(F32)
    query, cot = query_ref[...].astype(F32), cot_ref[...].astype(F32)
    products = jnp.concatenate([before_ref[...], (key * value).astype(BF16)], axis=0)
    forward = banded_pair(flipped_ref[...], above, lower)
    for b, mixed in enumerate(apply_filters(forward, products, blocks)):
        rows = slice(b * FILT, (b + 1) * FILT)
        output_ref[rows] = (query[rows] * mixed).astype(BF16)
        grad_query_ref[rows] = (cot[rows] * mixed).astype(BF16)
    grads = jnp.concatenate([(cot * query).astype(BF16), after_ref[...]], axis=0)
    backward = banded_pair(filt_ref[...], row <= col, row > col)
    for b, back in enumerate(apply_filters(backward, grads, blocks)):
        rows = slice(b * FILT, (b + 1) * FILT)
        grad_key_ref[rows] = (back * value[rows]).astype(BF16)
        grad_value_ref[rows] = (back * key[rows]).astype(BF16)


def finish_kernel(home_ref, rate_ref, grad_filter_ref, grad_rate_ref, *, scale):
    tap_count, group_count = grad_filter_ref.shape
    turned = home_ref[...].T
    first_tap = lax.axis_index("fsdp") * tap_count
    taps = (first_tap + iota((tap_count, group_count), 0)).astype(F32)
    rates = jnp.exp(rate_ref[...])
    grad_filter_ref[...] = turned[:tap_count, :group_count] * jnp.exp(-rates * taps) * scale
    grad_rate_ref[...] = turned[tap_count : tap_count + 1, :group_count] * (-rates) * scale


def params(mib=24):
    return pltpu.CompilerParams(vmem_limit_bytes=mib * MIB)


def moved_pieces(value, back):
    ctx, fsdp = lax.axis_size("ctx"), lax.axis_size("fsdp")
    pairs = []
    for c in range(ctx):
        for f in range(fsdp):
            there, column = landing(c, f)
            pairs.append((c * fsdp + f, there * fsdp + column))
    return lax.ppermute(value, ("ctx", "fsdp"), [(b, a) for a, b in pairs] if back else pairs)


def passed_along(value, by):
    peers = lax.axis_size("ctx")
    pairs = [(i, i + by) for i in range(peers) if 0 <= i + by < peers]
    return lax.ppermute(value, "ctx", pairs)


def per_device(query, key_in, value_in, cotangent, filter_weight, log_rate):
    tokens, channels = query.shape
    peers = lax.axis_size("ctx")
    groups = channels // GROUP
    scale = 1.0 / math.sqrt(tokens * peers * GROUP)
    rate_row = log_rate.reshape(1, -1)
    sds = jax.ShapeDtypeStruct
    last = tokens // FILT - 1
    tap_count, tap_groups = filter_weight.shape

    anywhere = pl.BlockSpec(memory_space=pl.ANY)
    edge = (FILT, channels)
    tail, head, taps = pl.pallas_call(
        front_kernel,
        in_specs=[anywhere] * 6,
        out_shape=[sds(edge, BF16), sds(edge, BF16), sds((tap_count, LANES), F32)],
        scratch_shapes=[pltpu.VMEM(filter_weight.shape, F32), pltpu.VMEM(rate_row.shape, F32)]
        + [pltpu.VMEM(edge, BF16)] * 4
        + [pltpu.SemaphoreType.DMA((6,))],
        compiler_params=params(60),
    )(key_in, value_in, query, cotangent, filter_weight, rate_row)
    after = passed_along(head, -1)
    taps_here = moved_pieces(taps, False)
    before = passed_along(tail, 1)

    tile = pl.BlockSpec((tokens, LANES), lambda i: (0, i))
    halo = pl.BlockSpec((FILT, LANES), lambda i: (0, i))
    group_rows = pl.BlockSpec((LANES // GROUP, LANES), lambda i: (i, 0))
    sums = pl.pallas_call(
        sums_kernel,
        out_shape=sds((groups, LANES), F32),
        compiler_params=params(),
    )(key_in, value_in, query, cotangent)
    sums = pl.pallas_call(
        whole_sums_kernel,
        out_shape=sds((groups, LANES), F32),
        compiler_params=params(),
    )(sums, tail, after)
    message = pl.pallas_call(
        message_kernel,
        out_shape=sds((peers, groups // 2 + tap_count, LANES), BF16),
        compiler_params=params(),
    )(sums, taps_here)
    received = lax.all_to_all(message, "ctx", 0, 0, tiled=True)
    filt, flipped, home = pl.pallas_call(
        reduce_kernel,
        out_shape=[sds((groups, LANES), F32), sds((groups, LANES), F32), sds((groups // 2, LANES), F32)],
        compiler_params=params(),
    )(received)
    home = moved_pieces(home, True)
    output, grad_query, grad_key, grad_value = pl.pallas_call(
        outputs_kernel,
        grid=(channels // LANES,),
        in_specs=[tile, tile, tile, tile, halo, halo, group_rows, group_rows],
        out_specs=[tile] * 4,
        out_shape=[sds((tokens, channels), BF16)] * 4,
        compiler_params=params(),
    )(key_in, value_in, query, cotangent, before, after, filt, flipped)
    grad_filter, grad_rate = pl.pallas_call(
        lambda *refs: finish_kernel(*refs, scale=scale),
        out_shape=[sds(filter_weight.shape, F32), sds(rate_row.shape, F32)],
        compiler_params=params(),
    )(home, rate_row)
    return (output, grad_query, grad_key, grad_value, grad_filter, grad_rate.reshape(log_rate.shape))


def solution(mesh):
    specs = (P("ctx", "fsdp"),) * 4 + (P("fsdp", "ctx"), P("ctx"))
    return jax.shard_map(per_device, mesh=mesh, in_specs=specs, out_specs=specs, check_vma=False)
```

```python
import math

import jax
import jax.numpy as jnp
from jax import lax
from jax.experimental import pallas as pl
from jax.experimental.pallas import tpu as pltpu
from jax.sharding import PartitionSpec as P

FILT = 128
GROUP = 16
LANES = 128
F32 = jnp.float32
BF16 = jnp.bfloat16
MIB = 1024 * 1024
NT = (((1,), (1,)), ((), ()))


def iota(shape, dim):
    return lax.broadcasted_iota(jnp.int32, shape, dim)


def rounded_product(a, b):
    return (a.astype(F32) * b.astype(F32)).astype(BF16)


def is_even():
    return lax.axis_index("ctx") % 2 == 0


def edge_rows(key, value, query, cot):
    tail, head = rounded_product(key, value), rounded_product(cot, query)
    return jnp.where(is_even(), tail, head), jnp.where(is_even(), head, tail)


def front_kernel(key, value, query, cot, weight, rate, near_ref, far_ref, taps_ref, *scratch):
    refs, sems = scratch[:-1], scratch[-1]
    tail = pl.ds(key.shape[0] - FILT, FILT)
    head = pl.ds(0, FILT)
    sources = [weight, rate, key.at[tail], value.at[tail], query.at[head], cot.at[head]]
    copies = [pltpu.make_async_copy(s, d, sems.at[i]) for i, (s, d) in enumerate(zip(sources, refs))]
    for copy in copies:
        copy.start()
    weight_ref, rate_ref = refs[:2]
    tap_count, group_count = weight.shape
    taps = (lax.axis_index("fsdp") * tap_count + iota((tap_count, group_count), 0)).astype(F32)
    taps_ref[...] = jnp.zeros_like(taps_ref)
    for copy in copies[:2]:
        copy.wait()
    decayed = weight_ref[...] * jnp.exp(-jnp.exp(rate_ref[...]) * taps)
    high = decayed.astype(BF16).astype(F32)
    taps_ref[:, :group_count] = high
    taps_ref[:, group_count : 2 * group_count] = decayed - high
    for copy in copies[2:]:
        copy.wait()
    near_ref[...], far_ref[...] = edge_rows(*(ref[...] for ref in refs[2:]))


def outer_products(left, right):
    groups = LANES // GROUP
    lane_group = (iota(left.shape, 1) % LANES) // GROUP
    zero = jnp.zeros_like(left)
    stacked = jnp.concatenate([jnp.where(lane_group == g, left, zero) for g in range(groups)], axis=0)
    outer = lax.dot_general(stacked, right, NT, preferred_element_type=F32)
    return [outer[g * FILT : (g + 1) * FILT] for g in range(groups)]


def diagonal_sums(squares):
    rolled = jnp.zeros((len(squares) * 8, LANES), F32)
    for i in range(FILT // 8):
        part = jnp.concatenate([m[8 * i : 8 * i + 8] for m in squares], axis=0)
        rolled = rolled + (pltpu.roll(part, FILT - 8 * i, axis=1) if i else part)
    row = iota(rolled.shape, 0) % 8
    for step in (1, 2, 4):
        rolled = jnp.where((row & step) != 0, pltpu.roll(rolled, FILT - step, axis=1), rolled)
    return rolled.reshape(len(squares), 8, LANES).sum(axis=1)


def same_block():
    return iota((FILT, FILT), 1) >= iota((FILT, FILT), 0)


def sums_kernel(key_ref, value_ref, query_ref, cot_ref, sums_ref):
    blocks = key_ref.shape[0] // FILT
    same = same_block()
    groups = LANES // GROUP
    for tile in range(key_ref.shape[1] // LANES):
        lanes = slice(tile * LANES, (tile + 1) * LANES)
        products = rounded_product(key_ref[:, lanes], value_ref[:, lanes])
        grads = rounded_product(cot_ref[:, lanes], query_ref[:, lanes])
        grads = jnp.concatenate([grads, jnp.zeros((FILT, LANES), BF16)], axis=0)
        left = jnp.concatenate([products[b * FILT : (b + 1) * FILT] for b in range(blocks)], axis=1)
        right = jnp.concatenate([grads[b * FILT : (b + 2) * FILT] for b in range(blocks)], axis=1)
        sums_ref[tile * groups : (tile + 1) * groups] = diagonal_sums(
            [jnp.where(same, outer[:, :FILT], outer[:, FILT:]) for outer in outer_products(left, right)]
        )


def whole_sums_kernel(sums_ref, own_near_ref, own_far_ref, far_ref, near_ref, out_ref):
    same = same_block()
    groups = LANES // GROUP
    for tile in range(own_near_ref.shape[1] // LANES):
        lanes = slice(tile * LANES, (tile + 1) * LANES)
        rows = slice(tile * groups, (tile + 1) * groups)
        tail = jnp.where(is_even(), own_near_ref[:, lanes], own_far_ref[:, lanes])
        after = jnp.where(is_even(), near_ref[:, lanes], far_ref[:, lanes])
        outers = outer_products(tail, after)
        crossing = diagonal_sums([jnp.where(same, jnp.zeros_like(outer), outer) for outer in outers])
        out_ref[rows] = sums_ref[rows] + crossing


def message_kernel(sums_ref, taps_ref, out_ref):
    half = sums_ref.shape[0] // 2
    taps = taps_ref[...]
    halves = [
        jnp.concatenate([sums_ref[h * half : (h + 1) * half], taps], axis=0).astype(BF16) for h in range(2)
    ]
    for peer in range(out_ref.shape[0]):
        out_ref[peer] = halves[peer % 2]


LANDING = ((0, 2, 3, 1), (0, 1, 2, 3), (0, 1, 2, 3), (2, 0, 1, 3))
SIDE = 4


def landing(ctx, fsdp):
    column, half = ctx // 2, ctx % 2
    x, hi = fsdp // SIDE, fsdp % SIDE
    place = (x + 2) % SIDE * SIDE + LANDING[column % SIDE][hi]
    return place * 2 + half, column


def by_column(column, values):
    out = values[1]
    for q in (0, 3):
        out = jnp.where(column % SIDE == q, values[q], out)
    return out


def landed_piece(ctx, column):
    low = ctx // 2 % SIDE
    hi = jnp.int32(0)
    for z in range(SIDE):
        hi = jnp.where(low == z, by_column(column, [jnp.int32(LANDING[q].index(z)) for q in range(SIDE)]), hi)
    return (ctx // 8 + 2) % SIDE * SIDE + hi


def reduce_kernel(recv_ref, filt_ref, flipped_ref, home_ref):
    peers = recv_ref.shape[0]
    half = GROUP
    own, column = lax.axis_index("ctx"), lax.axis_index("fsdp")
    total = jnp.zeros((half, LANES), F32)
    landed = []
    for peer in range(peers):
        message = recv_ref[peer].astype(F32)
        total = total + message[:half]
        landed.append(message[half:])
    eye = (iota((2 * half, LANES), 0) == iota((2 * half, LANES), 1)).astype(BF16)
    turned = []
    for h in range(2):
        pieces = []
        for piece in range(peers // 2):
            x, hi = piece // SIDE, piece % SIDE
            places = [(x + 2) % SIDE * SIDE + LANDING[q][hi] for q in range(SIDE)]
            pieces.append(by_column(column, [landed[2 * place + h] for place in places]))
        pieces = jnp.concatenate(pieces, axis=0).astype(BF16)
        turned.append(lax.dot_general(eye, pieces, NT, preferred_element_type=F32))
    high = jnp.concatenate([t[:half] for t in turned], axis=0)
    flip = ((iota((FILT, FILT), 0) + iota((FILT, FILT), 1)) % FILT == 0).astype(BF16)
    filt_ref[...] = high
    flipped_ref[...] = jnp.dot(high.astype(BF16), flip, preferred_element_type=F32)
    decayed = [t[:half] + t[half:] for t in turned]
    own_decayed = jnp.where(own % 2 == 0, decayed[0], decayed[1])
    lane = iota((half, LANES), 1)
    rate = jnp.sum(own_decayed * total * lane.astype(F32), axis=1, keepdims=True)
    tap_count = FILT * 2 // peers
    moved = pltpu.roll(total, (FILT - tap_count * landed_piece(own, column)) % FILT, axis=1)
    home_ref[...] = jnp.where(lane < tap_count, moved, rate)


def circulants(rows):
    return jnp.concatenate(
        [
            pltpu.roll(jnp.broadcast_to(rows[g : g + 1], (FILT, FILT)), 0, axis=1, stride=1, stride_axis=0)
            for g in range(rows.shape[0])
        ],
        axis=0,
    )


def banded_pair(rows, first, second):
    whole = circulants(rows)
    zero = jnp.zeros_like(whole)
    return jnp.concatenate([jnp.where(first, whole, zero), jnp.where(second, whole, zero)], axis=1).astype(BF16)


def apply_filters(band, padded, blocks):
    right = jnp.concatenate([padded[b * FILT : (b + 2) * FILT] for b in range(blocks)], axis=1)
    wide = jnp.dot(band, right, preferred_element_type=F32)
    lane_group = iota((FILT, LANES), 1) // GROUP
    out = []
    for b in range(blocks):
        kept = wide[:FILT, b * LANES : (b + 1) * LANES]
        for g in range(1, LANES // GROUP):
            kept = jnp.where(
                lane_group == g, wide[g * FILT : (g + 1) * FILT, b * LANES : (b + 1) * LANES], kept
            )
        out.append(kept)
    return out


def outputs_kernel(
    key_ref, value_ref, query_ref, cot_ref, far_ref, near_ref, filt_ref, flipped_ref,
    output_ref, grad_query_ref, grad_key_ref, grad_value_ref,
):
    blocks = key_ref.shape[0] // FILT
    groups = LANES // GROUP
    shape = (groups * FILT, FILT)
    row, col = iota(shape, 0) % FILT, iota(shape, 1)
    above, lower = row < col, row >= col
    key, value = key_ref[...].astype(F32), value_ref[...].astype(F32)
    query, cot = query_ref[...].astype(F32), cot_ref[...].astype(F32)
    before = jnp.where(is_even(), far_ref[...], near_ref[...])
    after = jnp.where(is_even(), near_ref[...], far_ref[...])
    products = jnp.concatenate([before, (key * value).astype(BF16)], axis=0)
    forward = banded_pair(flipped_ref[...], above, lower)
    for b, mixed in enumerate(apply_filters(forward, products, blocks)):
        rows = slice(b * FILT, (b + 1) * FILT)
        output_ref[rows] = (query[rows] * mixed).astype(BF16)
        grad_query_ref[rows] = (cot[rows] * mixed).astype(BF16)
    grads = jnp.concatenate([(cot * query).astype(BF16), after], axis=0)
    backward = banded_pair(filt_ref[...], row <= col, row > col)
    for b, back in enumerate(apply_filters(backward, grads, blocks)):
        rows = slice(b * FILT, (b + 1) * FILT)
        grad_key_ref[rows] = (back * value[rows]).astype(BF16)
        grad_value_ref[rows] = (back * key[rows]).astype(BF16)


def finish_kernel(home_ref, rate_ref, grad_filter_ref, grad_rate_ref, *, scale):
    tap_count, group_count = grad_filter_ref.shape
    turned = home_ref[...].T
    first_tap = lax.axis_index("fsdp") * tap_count
    taps = (first_tap + iota((tap_count, group_count), 0)).astype(F32)
    rates = jnp.exp(rate_ref[...])
    grad_filter_ref[...] = turned[:tap_count, :group_count] * jnp.exp(-rates * taps) * scale
    grad_rate_ref[...] = turned[tap_count : tap_count + 1, :group_count] * (-rates) * scale


def in_hbm(value):
    return pltpu.with_memory_space_constraint(value, pltpu.HBM)


def params(mib=24):
    return pltpu.CompilerParams(vmem_limit_bytes=mib * MIB)


def cost(us):
    return pl.CostEstimate(flops=int(us * 1e9), bytes_accessed=int(us * 3_000_000), transcendentals=0)


def moved_pieces(value, back):
    ctx, fsdp = lax.axis_size("ctx"), lax.axis_size("fsdp")
    pairs = []
    for c in range(ctx):
        for f in range(fsdp):
            there, column = landing(c, f)
            pairs.append((c * fsdp + f, there * fsdp + column))
    return lax.ppermute(value, ("ctx", "fsdp"), [(b, a) for a, b in pairs] if back else pairs)


def swapped(value, first):
    peers = lax.axis_size("ctx")
    pairs = []
    for i in range(first, peers - 1, 2):
        pairs += [(i, i + 1), (i + 1, i)]
    return lax.ppermute(value, "ctx", pairs)


def per_device(query, key_in, value_in, cotangent, filter_weight, log_rate):
    tokens, channels = query.shape
    peers = lax.axis_size("ctx")
    groups = channels // GROUP
    scale = 1.0 / math.sqrt(tokens * peers * GROUP)
    rate_row = log_rate.reshape(1, -1)
    sds = jax.ShapeDtypeStruct
    tap_count, tap_groups = filter_weight.shape

    edge = (FILT, channels)
    own_near, own_far, taps = pl.pallas_call(
        front_kernel,
        in_specs=[pl.BlockSpec(memory_space=pl.ANY)] * 6,
        out_shape=[sds(edge, BF16), sds(edge, BF16), sds((tap_count, LANES), F32)],
        scratch_shapes=[pltpu.VMEM(filter_weight.shape, F32), pltpu.VMEM(rate_row.shape, F32)]
        + [pltpu.VMEM(edge, BF16)] * 4
        + [pltpu.SemaphoreType.DMA((6,))],
        compiler_params=params(),
    )(*(in_hbm(x) for x in (key_in, value_in, query, cotangent, filter_weight, rate_row)))
    taps_here = moved_pieces(taps, False)
    far = swapped(own_far, 1)

    tile = pl.BlockSpec((tokens, LANES), lambda i: (0, i))
    halo = pl.BlockSpec((FILT, LANES), lambda i: (0, i))
    group_rows = pl.BlockSpec((LANES // GROUP, LANES), lambda i: (i, 0))
    sums = pl.pallas_call(
        sums_kernel,
        out_shape=sds((groups, LANES), F32),
        cost_estimate=cost(3), compiler_params=params(),
    )(key_in, value_in, query, cotangent)
    near = swapped(own_near, 0)
    sums = pl.pallas_call(
        whole_sums_kernel,
        out_shape=sds((groups, LANES), F32),
        compiler_params=params(),
    )(sums, own_near, own_far, far, near)
    message = pl.pallas_call(
        message_kernel,
        out_shape=pltpu.VMEM((peers, groups // 2 + tap_count, LANES), BF16),
        compiler_params=params(),
    )(sums, taps_here)
    received = lax.all_to_all(message, "ctx", 0, 0, tiled=True)
    filt, flipped, home = pl.pallas_call(
        reduce_kernel,
        out_shape=[sds((groups, LANES), F32), sds((groups, LANES), F32), sds((groups // 2, LANES), F32)],
        compiler_params=params(),
    )(received)
    home = moved_pieces(home, True)
    output, grad_query, grad_key, grad_value = pl.pallas_call(
        outputs_kernel,
        grid=(channels // LANES,),
        in_specs=[tile, tile, tile, tile, halo, halo, group_rows, group_rows],
        out_specs=[tile] * 4,
        out_shape=[sds((tokens, channels), BF16)] * 4,
        compiler_params=params(),
    )(key_in, value_in, query, cotangent, far, near, filt, flipped)
    grad_filter, grad_rate = pl.pallas_call(
        lambda *refs: finish_kernel(*refs, scale=scale),
        out_shape=[sds(filter_weight.shape, F32), sds(rate_row.shape, F32)],
        compiler_params=params(),
    )(home, rate_row)
    return (output, grad_query, grad_key, grad_value, grad_filter, grad_rate.reshape(log_rate.shape))


def solution(mesh):
    specs = (P("ctx", "fsdp"),) * 4 + (P("fsdp", "ctx"), P("ctx"))
    return jax.shard_map(per_device, mesh=mesh, in_specs=specs, out_specs=specs, check_vma=False)
```

```python
import math

import jax
import jax.numpy as jnp
from jax import lax
from jax.experimental import pallas as pl
from jax.experimental.pallas import tpu as pltpu
from jax.sharding import PartitionSpec as P

FILT = 128
GROUP = 16
LANES = 128
F32 = jnp.float32
BF16 = jnp.bfloat16
MIB = 1024 * 1024
NT = (((1,), (1,)), ((), ()))


def iota(shape, dim):
    return lax.broadcasted_iota(jnp.int32, shape, dim)


def flip_table():
    return ((iota((FILT, FILT), 0) + iota((FILT, FILT), 1)) % FILT == 0).astype(BF16)


def rounded_product(a, b):
    return (a.astype(F32) * b.astype(F32)).astype(BF16)


def front_kernel(key, value, query, cot, weight, rate, tail_ref, head_ref, taps_ref, *scratch):
    refs, sems = scratch[:-1], scratch[-1]
    tail = pl.ds(key.shape[0] - FILT, FILT)
    head = pl.ds(0, FILT)
    sources = [weight, rate, key.at[tail], value.at[tail], query.at[head], cot.at[head]]
    copies = [pltpu.make_async_copy(s, d, sems.at[i]) for i, (s, d) in enumerate(zip(sources, refs))]
    for copy in copies:
        copy.start()
    weight_ref, rate_ref = refs[:2]
    tap_count, group_count = weight.shape
    taps = (lax.axis_index("fsdp") * tap_count + iota((tap_count, group_count), 0)).astype(F32)
    taps_ref[...] = jnp.zeros_like(taps_ref)
    for copy in copies[:2]:
        copy.wait()
    decayed = weight_ref[...] * jnp.exp(-jnp.exp(rate_ref[...]) * taps)
    high = decayed.astype(BF16).astype(F32)
    taps_ref[:, :group_count] = high
    taps_ref[:, group_count : 2 * group_count] = decayed - high
    for copy in copies[2:]:
        copy.wait()
    key_ref, value_ref, query_ref, cot_ref = refs[2:]
    tail_ref[...] = rounded_product(key_ref[...], value_ref[...])
    head_ref[...] = rounded_product(cot_ref[...], query_ref[...])


def sums_kernel(key_ref, value_ref, query_ref, cot_ref, before_ref, sums_ref):
    blocks = key_ref.shape[0] // FILT
    groups = LANES // GROUP
    same = iota((FILT, FILT), 0) >= iota((FILT, FILT), 1)
    lane_group = (iota((FILT, blocks * LANES), 1) % LANES) // GROUP
    row = iota((groups * 8, LANES), 0) % 8
    sums = []
    for tile in range(key_ref.shape[1] // LANES):
        lanes = slice(tile * LANES, (tile + 1) * LANES)
        products = rounded_product(key_ref[:, lanes], value_ref[:, lanes])
        products = jnp.concatenate([before_ref[:, lanes], products], axis=0)
        grads = rounded_product(cot_ref[:, lanes], query_ref[:, lanes])
        left = jnp.concatenate([grads[b * FILT : (b + 1) * FILT] for b in range(blocks)], axis=1)
        right = jnp.concatenate([products[b * FILT : (b + 2) * FILT] for b in range(blocks)], axis=1)
        zero = jnp.zeros_like(left)
        stacked = jnp.concatenate([jnp.where(lane_group == g, left, zero) for g in range(groups)], axis=0)
        outer = lax.dot_general(stacked, right, NT, preferred_element_type=F32)
        squares = []
        for g in range(groups):
            rows = slice(g * FILT, (g + 1) * FILT)
            squares.append(jnp.where(same, outer[rows, FILT:], outer[rows, :FILT]))
        rolled = jnp.zeros((groups * 8, LANES), F32)
        for i in range(FILT // 8):
            part = jnp.concatenate([m[8 * i : 8 * i + 8] for m in squares], axis=0)
            rolled = rolled + (pltpu.roll(part, FILT - 8 * i, axis=1) if i else part)
        for step in (1, 2, 4):
            rolled = jnp.where((row & step) != 0, pltpu.roll(rolled, FILT - step, axis=1), rolled)
        sums.append(rolled.reshape(groups, 8, LANES).sum(axis=1))
    backwards = jnp.concatenate(sums, axis=0).astype(BF16)
    sums_ref[...] = jnp.dot(backwards, flip_table(), preferred_element_type=F32)


def message_kernel(sums_ref, taps_ref, out_ref):
    half = sums_ref.shape[0] // 2
    taps = taps_ref[...]
    halves = [
        jnp.concatenate([sums_ref[h * half : (h + 1) * half], taps], axis=0).astype(BF16) for h in range(2)
    ]
    for peer in range(out_ref.shape[0]):
        out_ref[peer] = halves[peer % 2]


LANDING = ((0, 2, 3, 1), (0, 1, 2, 3), (0, 1, 2, 3), (2, 0, 1, 3))
SIDE = 4


def landing(ctx, fsdp):
    column, half = ctx // 2, ctx % 2
    x, hi = fsdp // SIDE, fsdp % SIDE
    place = (x + 2) % SIDE * SIDE + LANDING[column % SIDE][hi]
    return place * 2 + half, column


def by_column(column, values):
    out = values[1]
    for q in (0, 3):
        out = jnp.where(column % SIDE == q, values[q], out)
    return out


def landed_piece(ctx, column):
    low = ctx // 2 % SIDE
    hi = jnp.int32(0)
    for z in range(SIDE):
        hi = jnp.where(low == z, by_column(column, [jnp.int32(LANDING[q].index(z)) for q in range(SIDE)]), hi)
    return (ctx // 8 + 2) % SIDE * SIDE + hi


def reduce_kernel(recv_ref, filt_ref, flipped_ref, home_ref):
    peers = recv_ref.shape[0]
    half = GROUP
    own, column = lax.axis_index("ctx"), lax.axis_index("fsdp")
    total = jnp.zeros((half, LANES), F32)
    landed = []
    for peer in range(peers):
        message = recv_ref[peer].astype(F32)
        total = total + message[:half]
        landed.append(message[half:])
    eye = (iota((2 * half, LANES), 0) == iota((2 * half, LANES), 1)).astype(BF16)
    turned = []
    for h in range(2):
        pieces = []
        for piece in range(peers // 2):
            x, hi = piece // SIDE, piece % SIDE
            places = [(x + 2) % SIDE * SIDE + LANDING[q][hi] for q in range(SIDE)]
            pieces.append(by_column(column, [landed[2 * place + h] for place in places]))
        pieces = jnp.concatenate(pieces, axis=0).astype(BF16)
        turned.append(lax.dot_general(eye, pieces, NT, preferred_element_type=F32))
    high = jnp.concatenate([t[:half] for t in turned], axis=0)
    filt_ref[...] = high
    flipped_ref[...] = jnp.dot(high.astype(BF16), flip_table(), preferred_element_type=F32)
    decayed = [t[:half] + t[half:] for t in turned]
    own_decayed = jnp.where(own % 2 == 0, decayed[0], decayed[1])
    lane = iota((half, LANES), 1)
    rate = jnp.sum(own_decayed * total * lane.astype(F32), axis=1, keepdims=True)
    tap_count = FILT * 2 // peers
    moved = pltpu.roll(total, (FILT - tap_count * landed_piece(own, column)) % FILT, axis=1)
    home_ref[...] = jnp.where(lane < tap_count, moved, rate)


def circulants(rows):
    return jnp.concatenate(
        [
            pltpu.roll(jnp.broadcast_to(rows[g : g + 1], (FILT, FILT)), 0, axis=1, stride=1, stride_axis=0)
            for g in range(rows.shape[0])
        ],
        axis=0,
    )


def banded_pair(rows, first, second):
    whole = circulants(rows)
    zero = jnp.zeros_like(whole)
    return jnp.concatenate([jnp.where(first, whole, zero), jnp.where(second, whole, zero)], axis=1).astype(BF16)


def apply_filters(band, padded, blocks):
    groups, step = LANES // GROUP, 32
    right = jnp.concatenate([padded[b * FILT : (b + 2) * FILT] for b in range(blocks)], axis=1)
    lane_group = iota((step, LANES), 1) // GROUP
    parts = [[] for _ in range(blocks)]
    for first in range(0, FILT, step):
        left = jnp.concatenate([band[g * FILT + first : g * FILT + first + step] for g in range(groups)], axis=0)
        wide = jnp.dot(left, right, preferred_element_type=F32)
        for b in range(blocks):
            lanes = slice(b * LANES, (b + 1) * LANES)
            kept = wide[:step, lanes]
            for g in range(1, groups):
                kept = jnp.where(lane_group == g, wide[g * step : (g + 1) * step, lanes], kept)
            parts[b].append(kept)
    return [jnp.concatenate(p, axis=0) for p in parts]


def outputs_kernel(
    key_ref, value_ref, query_ref, cot_ref, before_ref, after_ref, filt_ref, flipped_ref, *rest
):
    places, buffers, sems = rest[:4], rest[4:8], rest[8]
    blocks = key_ref.shape[0] // FILT
    groups = LANES // GROUP
    shape = (groups * FILT, FILT)
    row, col = iota(shape, 0) % FILT, iota(shape, 1)
    copies = []

    def send(index, tile):
        lanes = pl.ds(tile * LANES, LANES)
        copy = pltpu.make_async_copy(
            buffers[index].at[:, lanes], places[index].at[:, lanes], sems.at[len(copies)]
        )
        copy.start()
        copies.append(copy)

    for tile in range(key_ref.shape[1] // LANES):
        lanes = slice(tile * LANES, (tile + 1) * LANES)
        own = slice(tile * groups, (tile + 1) * groups)
        key, value = key_ref[:, lanes].astype(F32), value_ref[:, lanes].astype(F32)
        query, cot = query_ref[:, lanes].astype(F32), cot_ref[:, lanes].astype(F32)
        products = jnp.concatenate([before_ref[:, lanes], (key * value).astype(BF16)], axis=0)
        forward = banded_pair(flipped_ref[own], row < col, row >= col)
        for b, mixed in enumerate(apply_filters(forward, products, blocks)):
            rows = slice(b * FILT, (b + 1) * FILT)
            buffers[0][rows, lanes] = (query[rows] * mixed).astype(BF16)
            buffers[1][rows, lanes] = (cot[rows] * mixed).astype(BF16)
        send(0, tile)
        send(1, tile)
        grads = jnp.concatenate([(cot * query).astype(BF16), after_ref[:, lanes]], axis=0)
        backward = banded_pair(filt_ref[own], row <= col, row > col)
        for b, back in enumerate(apply_filters(backward, grads, blocks)):
            rows = slice(b * FILT, (b + 1) * FILT)
            buffers[2][rows, lanes] = (back * value[rows]).astype(BF16)
            buffers[3][rows, lanes] = (back * key[rows]).astype(BF16)
        send(2, tile)
        send(3, tile)
    for copy in copies:
        copy.wait()


def finish_kernel(home_ref, rate_ref, grad_filter_ref, grad_rate_ref, *, scale):
    tap_count, group_count = grad_filter_ref.shape
    turned = home_ref[...].T
    first_tap = lax.axis_index("fsdp") * tap_count
    taps = (first_tap + iota((tap_count, group_count), 0)).astype(F32)
    rates = jnp.exp(rate_ref[...])
    grad_filter_ref[...] = turned[:tap_count, :group_count] * jnp.exp(-rates * taps) * scale
    grad_rate_ref[...] = turned[tap_count : tap_count + 1, :group_count] * (-rates) * scale


def in_hbm(value):
    return pltpu.with_memory_space_constraint(value, pltpu.HBM)


def params(mib=24):
    return pltpu.CompilerParams(vmem_limit_bytes=mib * MIB)


def cost(us):
    return pl.CostEstimate(flops=int(us * 1e9), bytes_accessed=int(us * 3_000_000), transcendentals=0)


def moved_pieces(value, back):
    ctx, fsdp = lax.axis_size("ctx"), lax.axis_size("fsdp")
    pairs = []
    for c in range(ctx):
        for f in range(fsdp):
            there, column = landing(c, f)
            pairs.append((c * fsdp + f, there * fsdp + column))
    return lax.ppermute(value, ("ctx", "fsdp"), [(b, a) for a, b in pairs] if back else pairs)


def passed_along(value, by):
    peers = lax.axis_size("ctx")
    pairs = [(i, i + by) for i in range(peers) if 0 <= i + by < peers]
    return lax.ppermute(value, "ctx", pairs)


def per_device(query, key_in, value_in, cotangent, filter_weight, log_rate):
    tokens, channels = query.shape
    peers = lax.axis_size("ctx")
    groups = channels // GROUP
    scale = 1.0 / math.sqrt(tokens * peers * GROUP)
    rate_row = log_rate.reshape(1, -1)
    sds = jax.ShapeDtypeStruct
    tap_count, tap_groups = filter_weight.shape

    edge = (FILT, channels)
    anywhere = pl.BlockSpec(memory_space=pl.ANY)
    tail, head, taps = pl.pallas_call(
        front_kernel,
        in_specs=[anywhere] * 6,
        out_shape=[sds(edge, BF16), sds(edge, BF16), sds((tap_count, LANES), F32)],
        scratch_shapes=[pltpu.VMEM(filter_weight.shape, F32), pltpu.VMEM(rate_row.shape, F32)]
        + [pltpu.VMEM(edge, BF16)] * 4
        + [pltpu.SemaphoreType.DMA((6,))],
        compiler_params=params(),
    )(*(in_hbm(x) for x in (key_in, value_in, query, cotangent, filter_weight, rate_row)))
    taps_here = moved_pieces(taps, False)
    before = passed_along(tail, 1)
    after = passed_along(head, -1)

    sums = pl.pallas_call(
        sums_kernel,
        out_shape=sds((groups, LANES), F32),
        cost_estimate=cost(0.5),
        compiler_params=params(),
    )(key_in, value_in, query, cotangent, before)
    message = pl.pallas_call(
        message_kernel,
        out_shape=sds((peers, groups // 2 + tap_count, LANES), BF16),
        compiler_params=params(),
    )(sums, taps_here)
    received = lax.all_to_all(message, "ctx", 0, 0, tiled=True)
    filt, flipped, home = pl.pallas_call(
        reduce_kernel,
        out_shape=[sds((groups, LANES), F32), sds((groups, LANES), F32), sds((groups // 2, LANES), F32)],
        compiler_params=params(),
    )(received)
    home = moved_pieces(home, True)
    output, grad_query, grad_key, grad_value = pl.pallas_call(
        outputs_kernel,
        out_specs=[anywhere] * 4,
        out_shape=[sds((tokens, channels), BF16)] * 4,
        scratch_shapes=[pltpu.VMEM((tokens, channels), BF16)] * 4
        + [pltpu.SemaphoreType.DMA((4 * channels // LANES,))],
        compiler_params=params(),
    )(key_in, value_in, query, cotangent, before, after, filt, flipped)
    grad_filter, grad_rate = pl.pallas_call(
        lambda *refs: finish_kernel(*refs, scale=scale),
        out_shape=[sds(filter_weight.shape, F32), sds(rate_row.shape, F32)],
        compiler_params=params(),
    )(home, rate_row)
    return (output, grad_query, grad_key, grad_value, grad_filter, grad_rate.reshape(log_rate.shape))


def solution(mesh):
    specs = (P("ctx", "fsdp"),) * 4 + (P("fsdp", "ctx"), P("ctx"))
    return jax.shard_map(per_device, mesh=mesh, in_specs=specs, out_specs=specs, check_vma=False)
```

```python
import math

import jax
import jax.numpy as jnp
from jax import lax
from jax.experimental import pallas as pl
from jax.experimental.pallas import tpu as pltpu
from jax.sharding import PartitionSpec as P

FILT = 128
GROUP = 16
LANES = 128
F32 = jnp.float32
BF16 = jnp.bfloat16
MIB = 1024 * 1024
NT = (((1,), (1,)), ((), ()))


def iota(shape, dim):
    return lax.broadcasted_iota(jnp.int32, shape, dim)


def flip_table():
    return ((iota((FILT, FILT), 0) + iota((FILT, FILT), 1)) % FILT == 0).astype(BF16)


def rounded_product(a, b):
    return (a.astype(F32) * b.astype(F32)).astype(BF16)


def front_kernel(key, value, query, cot, weight, rate, tail_ref, late_tail_ref, taps_ref, *scratch):
    refs, sems = scratch[:-1], scratch[-1]
    tail = pl.ds(key.shape[0] - FILT, FILT)
    sources = [weight, rate, key.at[tail], value.at[tail]]
    copies = [pltpu.make_async_copy(s, d, sems.at[i]) for i, (s, d) in enumerate(zip(sources, refs))]
    for copy in copies:
        copy.start()
    weight_ref, rate_ref = refs[:2]
    tap_count, group_count = weight.shape
    taps = (lax.axis_index("fsdp") * tap_count + iota((tap_count, group_count), 0)).astype(F32)
    taps_ref[...] = jnp.zeros_like(taps_ref)
    for copy in copies[:2]:
        copy.wait()
    decayed = weight_ref[...] * jnp.exp(-jnp.exp(rate_ref[...]) * taps)
    high = decayed.astype(BF16).astype(F32)
    taps_ref[:, :group_count] = high
    taps_ref[:, group_count : 2 * group_count] = decayed - high
    for copy in copies[2:]:
        copy.wait()
    products = rounded_product(refs[2][...], refs[3][...])
    tail_ref[...] = products
    late_tail_ref[...] = products


LANDING = ((0, 2, 3, 1), (0, 1, 2, 3), (0, 1, 2, 3), (2, 0, 1, 3))
SIDE = 4


def is_late():
    return lax.axis_index("fsdp") % SIDE != 0


HALF = LANES // 2


def packed_halves(blocks_list):
    low = iota((FILT, LANES), 1) < HALF
    turned = [pltpu.roll(x, HALF, axis=1) for x in blocks_list]

    def pair(half, i, j):
        first, second = (blocks_list[i], turned[j]) if half == 0 else (turned[i], blocks_list[j])
        return jnp.where(low, first, second)

    return pair


def diagonal_sums(left, right, period):
    step, groups = FILT // 2, period // GROUP
    lane_group = (iota((step, left.shape[1]), 1) % period) // GROUP
    zero = jnp.zeros((step, left.shape[1]), BF16)
    total = jnp.zeros((groups * 8, LANES), F32)
    for first in range(0, FILT, step):
        rows = left[first : first + step]
        stacked = jnp.concatenate([jnp.where(lane_group == g, rows, zero) for g in range(groups)], axis=0)
        outer = lax.dot_general(stacked, right, NT, preferred_element_type=F32)
        for i in range(first, first + step, 8):
            same = iota((8, FILT), 0) + i >= iota((8, FILT), 1)
            parts = []
            for g in range(groups):
                row = slice(g * step + i - first, g * step + i - first + 8)
                before = outer[row, :FILT]
                own = outer[row, FILT:] if right.shape[0] > FILT else jnp.zeros_like(before)
                parts.append(jnp.where(same, own, before))
            part = jnp.concatenate(parts, axis=0)
            total = total + (pltpu.roll(part, FILT - i, axis=1) if i else part)
    row = iota(total.shape, 0) % 8
    for step in (1, 2, 4):
        total = jnp.where((row & step) != 0, pltpu.roll(total, FILT - step, axis=1), total)
    return total.reshape(groups, 8, LANES).sum(axis=1)


def sums_kernel(key_ref, value_ref, query_ref, cot_ref, before_ref, sums_ref, head_ref):
    blocks = key_ref.shape[0] // FILT
    sums = []
    for tile in range(key_ref.shape[1] // LANES):
        lanes = slice(tile * LANES, (tile + 1) * LANES)
        products = rounded_product(key_ref[:, lanes], value_ref[:, lanes])
        grads = rounded_product(cot_ref[:, lanes], query_ref[:, lanes])
        head_ref[:, lanes] = grads[:FILT]
        ours = packed_halves([grads[b * FILT : (b + 1) * FILT] for b in range(blocks)])
        theirs = packed_halves(
            [before_ref[:, lanes]] + [products[b * FILT : (b + 1) * FILT] for b in range(blocks)]
        )
        pairs = range(0, blocks, 2)
        for half in range(2):
            left = jnp.concatenate([ours(half, b, b + 1) for b in pairs], axis=1)
            earlier = jnp.concatenate([theirs(half, b, b + 1) for b in pairs], axis=1)
            own = jnp.concatenate([theirs(half, b + 1, b + 2) for b in pairs], axis=1)
            sums.append(diagonal_sums(left, jnp.concatenate([earlier, own], axis=0), HALF))
    sums_ref[...] = jnp.concatenate(sums, axis=0)


def ordered_kernel(sums_ref, before_ref, head_ref, out_ref, total_ref):
    total_ref[...] = sums_ref[...]

    @pl.when(is_late())
    def _():
        groups = LANES // GROUP
        for tile in range(head_ref.shape[1] // LANES):
            lanes = slice(tile * LANES, (tile + 1) * LANES)
            rows = slice(tile * groups, (tile + 1) * groups)
            total_ref[rows] = total_ref[rows] + diagonal_sums(head_ref[:, lanes], before_ref[:, lanes], LANES)

    out_ref[...] = jnp.dot(total_ref[...].astype(BF16), flip_table(), preferred_element_type=F32)


def message_kernel(sums_ref, taps_ref, out_ref):
    half = sums_ref.shape[0] // 2
    taps = taps_ref[...]
    halves = [
        jnp.concatenate([sums_ref[h * half : (h + 1) * half], taps], axis=0).astype(BF16) for h in range(2)
    ]
    for peer in range(out_ref.shape[0]):
        out_ref[peer] = halves[peer % 2]


def landing(ctx, fsdp):
    column, half = ctx // 2, ctx % 2
    x, hi = fsdp // SIDE, fsdp % SIDE
    place = (x + 2) % SIDE * SIDE + LANDING[column % SIDE][hi]
    return place * 2 + half, column


def by_column(column, values):
    out = values[1]
    for q in (0, 3):
        out = jnp.where(column % SIDE == q, values[q], out)
    return out


def landed_piece(ctx, column):
    low = ctx // 2 % SIDE
    hi = jnp.int32(0)
    for z in range(SIDE):
        hi = jnp.where(low == z, by_column(column, [jnp.int32(LANDING[q].index(z)) for q in range(SIDE)]), hi)
    return (ctx // 8 + 2) % SIDE * SIDE + hi


def reduce_kernel(recv_ref, filt_ref, flipped_ref, home_ref):
    peers = recv_ref.shape[0]
    half = GROUP
    own, column = lax.axis_index("ctx"), lax.axis_index("fsdp")
    total = jnp.zeros((half, LANES), F32)
    landed = []
    for peer in range(peers):
        message = recv_ref[peer].astype(F32)
        total = total + message[:half]
        landed.append(message[half:])
    eye = (iota((2 * half, LANES), 0) == iota((2 * half, LANES), 1)).astype(BF16)
    turned = []
    for h in range(2):
        pieces = []
        for piece in range(peers // 2):
            x, hi = piece // SIDE, piece % SIDE
            places = [(x + 2) % SIDE * SIDE + LANDING[q][hi] for q in range(SIDE)]
            pieces.append(by_column(column, [landed[2 * place + h] for place in places]))
        pieces = jnp.concatenate(pieces, axis=0).astype(BF16)
        turned.append(lax.dot_general(eye, pieces, NT, preferred_element_type=F32))
    high = jnp.concatenate([t[:half] for t in turned], axis=0)
    filt_ref[...] = high
    flipped_ref[...] = jnp.dot(high.astype(BF16), flip_table(), preferred_element_type=F32)
    decayed = [t[:half] + t[half:] for t in turned]
    own_decayed = jnp.where(own % 2 == 0, decayed[0], decayed[1])
    lane = iota((half, LANES), 1)
    rate = jnp.sum(own_decayed * total * lane.astype(F32), axis=1, keepdims=True)
    tap_count = FILT * 2 // peers
    moved = pltpu.roll(total, (FILT - tap_count * landed_piece(own, column)) % FILT, axis=1)
    home_ref[...] = jnp.where(lane < tap_count, moved, rate)


def circulants(rows):
    return jnp.concatenate(
        [
            pltpu.roll(jnp.broadcast_to(rows[g : g + 1], (FILT, FILT)), 0, axis=1, stride=1, stride_axis=0)
            for g in range(rows.shape[0])
        ],
        axis=0,
    )


def banded_pair(rows, first, second):
    whole = circulants(rows)
    zero = jnp.zeros_like(whole)
    return jnp.concatenate([jnp.where(first, whole, zero), jnp.where(second, whole, zero)], axis=1).astype(BF16)


def apply_filters(band, padded, blocks):
    groups, step = LANES // GROUP, 32
    right = jnp.concatenate([padded[b * FILT : (b + 2) * FILT] for b in range(blocks)], axis=1)
    lane_group = iota((step, LANES), 1) // GROUP
    parts = [[] for _ in range(blocks)]
    for first in range(0, FILT, step):
        left = jnp.concatenate([band[g * FILT + first : g * FILT + first + step] for g in range(groups)], axis=0)
        wide = jnp.dot(left, right, preferred_element_type=F32)
        for b in range(blocks):
            lanes = slice(b * LANES, (b + 1) * LANES)
            kept = wide[:step, lanes]
            for g in range(1, groups):
                kept = jnp.where(lane_group == g, wide[g * step : (g + 1) * step, lanes], kept)
            parts[b].append(kept)
    return [jnp.concatenate(p, axis=0) for p in parts]


def outputs_kernel(
    key_ref, value_ref, query_ref, cot_ref, early_ref, late_ref, after_ref, filt_ref, flipped_ref, *rest
):
    places, buffers, sems = rest[:4], rest[4:8], rest[8]
    blocks = key_ref.shape[0] // FILT
    groups = LANES // GROUP
    shape = (groups * FILT, FILT)
    row, col = iota(shape, 0) % FILT, iota(shape, 1)
    copies = []

    def send(index, tile):
        lanes = pl.ds(tile * LANES, LANES)
        copy = pltpu.make_async_copy(
            buffers[index].at[:, lanes], places[index].at[:, lanes], sems.at[len(copies)]
        )
        copy.start()
        copies.append(copy)

    for tile in range(key_ref.shape[1] // LANES):
        lanes = slice(tile * LANES, (tile + 1) * LANES)
        own = slice(tile * groups, (tile + 1) * groups)
        key, value = key_ref[:, lanes].astype(F32), value_ref[:, lanes].astype(F32)
        query, cot = query_ref[:, lanes].astype(F32), cot_ref[:, lanes].astype(F32)
        before = jnp.where(is_late(), late_ref[:, lanes], early_ref[:, lanes])
        products = jnp.concatenate([before, (key * value).astype(BF16)], axis=0)
        forward = banded_pair(flipped_ref[own], row < col, row >= col)
        for b, mixed in enumerate(apply_filters(forward, products, blocks)):
            rows = slice(b * FILT, (b + 1) * FILT)
            buffers[0][rows, lanes] = (query[rows] * mixed).astype(BF16)
            buffers[1][rows, lanes] = (cot[rows] * mixed).astype(BF16)
        send(0, tile)
        send(1, tile)
        grads = jnp.concatenate([(cot * query).astype(BF16), after_ref[:, lanes]], axis=0)
        backward = banded_pair(filt_ref[own], row <= col, row > col)
        for b, back in enumerate(apply_filters(backward, grads, blocks)):
            rows = slice(b * FILT, (b + 1) * FILT)
            buffers[2][rows, lanes] = (back * value[rows]).astype(BF16)
            buffers[3][rows, lanes] = (back * key[rows]).astype(BF16)
        send(2, tile)
        send(3, tile)
    for copy in copies:
        copy.wait()


def finish_kernel(home_ref, rate_ref, grad_filter_ref, grad_rate_ref, *, scale):
    tap_count, group_count = grad_filter_ref.shape
    turned = home_ref[...].T
    first_tap = lax.axis_index("fsdp") * tap_count
    taps = (first_tap + iota((tap_count, group_count), 0)).astype(F32)
    rates = jnp.exp(rate_ref[...])
    grad_filter_ref[...] = turned[:tap_count, :group_count] * jnp.exp(-rates * taps) * scale
    grad_rate_ref[...] = turned[tap_count : tap_count + 1, :group_count] * (-rates) * scale


def in_hbm(value):
    return pltpu.with_memory_space_constraint(value, pltpu.HBM)


def params(mib=24):
    return pltpu.CompilerParams(vmem_limit_bytes=mib * MIB)


def cost(us):
    return pl.CostEstimate(flops=int(us * 1e9), bytes_accessed=int(us * 3_000_000), transcendentals=0)


def moved_pieces(value, back):
    ctx, fsdp = lax.axis_size("ctx"), lax.axis_size("fsdp")
    pairs = []
    for c in range(ctx):
        for f in range(fsdp):
            there, column = landing(c, f)
            pairs.append((c * fsdp + f, there * fsdp + column))
    return lax.ppermute(value, ("ctx", "fsdp"), [(b, a) for a, b in pairs] if back else pairs)


def passed_along(value, by, chosen=lambda column: True):
    ctx, fsdp = lax.axis_size("ctx"), lax.axis_size("fsdp")
    pairs = [
        (c * fsdp + f, (c + by) * fsdp + f)
        for c in range(ctx) for f in range(fsdp) if 0 <= c + by < ctx and chosen(f)
    ]
    return lax.ppermute(value, ("ctx", "fsdp"), pairs)


def per_device(query, key_in, value_in, cotangent, filter_weight, log_rate):
    tokens, channels = query.shape
    peers = lax.axis_size("ctx")
    groups = channels // GROUP
    scale = 1.0 / math.sqrt(tokens * peers * GROUP)
    rate_row = log_rate.reshape(1, -1)
    sds = jax.ShapeDtypeStruct
    tap_count, tap_groups = filter_weight.shape

    edge = (FILT, channels)
    anywhere = pl.BlockSpec(memory_space=pl.ANY)
    tail, late_tail, taps = pl.pallas_call(
        front_kernel,
        in_specs=[anywhere] * 6,
        out_shape=[sds(edge, BF16)] * 2 + [sds((tap_count, LANES), F32)],
        scratch_shapes=[pltpu.VMEM(filter_weight.shape, F32), pltpu.VMEM(rate_row.shape, F32)]
        + [pltpu.VMEM(edge, BF16)] * 2
        + [pltpu.SemaphoreType.DMA((4,))],
        compiler_params=params(),
    )(*(in_hbm(x) for x in (key_in, value_in, query, cotangent, filter_weight, rate_row)))
    taps_here = moved_pieces(taps, False)
    early = passed_along(tail, 1, lambda f: f % SIDE == 0)
    late = passed_along(late_tail, 1, lambda f: f % SIDE != 0)

    sums, head = pl.pallas_call(
        sums_kernel,
        out_shape=[sds((groups, LANES), F32), sds(edge, BF16)],
        cost_estimate=cost(3),
        compiler_params=params(),
    )(key_in, value_in, query, cotangent, early)
    after = passed_along(head, -1)
    sums = pl.pallas_call(
        ordered_kernel,
        out_shape=sds((groups, LANES), F32),
        scratch_shapes=[pltpu.VMEM((groups, LANES), F32)],
        compiler_params=params(),
    )(sums, late, head)
    message = pl.pallas_call(
        message_kernel,
        out_shape=sds((peers, groups // 2 + tap_count, LANES), BF16),
        compiler_params=params(),
    )(sums, taps_here)
    received = lax.all_to_all(message, "ctx", 0, 0, tiled=True)
    filt, flipped, home = pl.pallas_call(
        reduce_kernel,
        out_shape=[sds((groups, LANES), F32), sds((groups, LANES), F32), sds((groups // 2, LANES), F32)],
        compiler_params=params(),
    )(received)
    home = moved_pieces(home, True)
    output, grad_query, grad_key, grad_value = pl.pallas_call(
        outputs_kernel,
        out_specs=[anywhere] * 4,
        out_shape=[sds((tokens, channels), BF16)] * 4,
        scratch_shapes=[pltpu.VMEM((tokens, channels), BF16)] * 4
        + [pltpu.SemaphoreType.DMA((4 * channels // LANES,))],
        compiler_params=params(),
    )(key_in, value_in, query, cotangent, early, late, after, filt, flipped)
    grad_filter, grad_rate = pl.pallas_call(
        lambda *refs: finish_kernel(*refs, scale=scale),
        out_shape=[sds(filter_weight.shape, F32), sds(rate_row.shape, F32)],
        compiler_params=params(),
    )(home, rate_row)
    return (output, grad_query, grad_key, grad_value, grad_filter, grad_rate.reshape(log_rate.shape))


def solution(mesh):
    specs = (P("ctx", "fsdp"),) * 4 + (P("fsdp", "ctx"), P("ctx"))
    return jax.shard_map(per_device, mesh=mesh, in_specs=specs, out_specs=specs, check_vma=False)
```

```python
import math

import jax
import jax.numpy as jnp
from jax import lax
from jax.experimental import pallas as pl
from jax.experimental.pallas import tpu as pltpu
from jax.sharding import PartitionSpec as P

FILT = 128
GROUP = 16
LANES = 128
F32 = jnp.float32
BF16 = jnp.bfloat16
MIB = 1024 * 1024
NT = (((1,), (1,)), ((), ()))


def iota(shape, dim):
    return lax.broadcasted_iota(jnp.int32, shape, dim)


def flip_table():
    return ((iota((FILT, FILT), 0) + iota((FILT, FILT), 1)) % FILT == 0).astype(BF16)


def rounded_product(a, b):
    return (a.astype(F32) * b.astype(F32)).astype(BF16)


def front_kernel(key, value, query, cot, weight, rate, tail_ref, taps_ref, *scratch):
    refs, sems = scratch[:-1], scratch[-1]
    tail = pl.ds(key.shape[0] - FILT, FILT)
    sources = [weight, rate, key.at[tail], value.at[tail]]
    copies = [pltpu.make_async_copy(s, d, sems.at[i]) for i, (s, d) in enumerate(zip(sources, refs))]
    for copy in copies[:2]:
        copy.start()

    @pl.when(jnp.logical_not(is_late()))
    def _():
        for copy in copies[2:]:
            copy.start()

    weight_ref, rate_ref = refs[:2]
    tap_count, group_count = weight.shape
    taps = (lax.axis_index("fsdp") * tap_count + iota((tap_count, group_count), 0)).astype(F32)
    taps_ref[...] = jnp.zeros_like(taps_ref)
    for copy in copies[:2]:
        copy.wait()
    decayed = weight_ref[...] * jnp.exp(-jnp.exp(rate_ref[...]) * taps)
    high = decayed.astype(BF16).astype(F32)
    taps_ref[:, :group_count] = high
    taps_ref[:, group_count : 2 * group_count] = decayed - high

    @pl.when(jnp.logical_not(is_late()))
    def _():
        for copy in copies[2:]:
            copy.wait()
        tail_ref[...] = rounded_product(refs[2][...], refs[3][...])


def tail_kernel(key_ref, value_ref, tail_ref):
    tail_ref[...] = rounded_product(key_ref[-FILT:], value_ref[-FILT:])


LANDING = ((0, 2, 3, 1), (0, 1, 2, 3), (0, 1, 2, 3), (2, 0, 1, 3))
SIDE = 4


def is_late():
    return lax.axis_index("fsdp") % SIDE != 0


HALF = LANES // 2


def packed_halves(blocks_list):
    low = iota((FILT, LANES), 1) < HALF
    turned = [pltpu.roll(x, HALF, axis=1) for x in blocks_list]

    def pair(half, i, j):
        first, second = (blocks_list[i], turned[j]) if half == 0 else (turned[i], blocks_list[j])
        return jnp.where(low, first, second)

    return pair


def diagonal_sums(left, right, period):
    step, groups = FILT // 2, period // GROUP
    lane_group = (iota((step, left.shape[1]), 1) % period) // GROUP
    zero = jnp.zeros((step, left.shape[1]), BF16)
    total = jnp.zeros((groups * 8, LANES), F32)
    for first in range(0, FILT, step):
        rows = left[first : first + step]
        stacked = jnp.concatenate([jnp.where(lane_group == g, rows, zero) for g in range(groups)], axis=0)
        outer = lax.dot_general(stacked, right, NT, preferred_element_type=F32)
        for i in range(first, first + step, 8):
            same = iota((8, FILT), 0) + i >= iota((8, FILT), 1)
            parts = []
            for g in range(groups):
                row = slice(g * step + i - first, g * step + i - first + 8)
                before = outer[row, :FILT]
                own = outer[row, FILT:] if right.shape[0] > FILT else jnp.zeros_like(before)
                parts.append(jnp.where(same, own, before))
            part = jnp.concatenate(parts, axis=0)
            total = total + (pltpu.roll(part, FILT - i, axis=1) if i else part)
    row = iota(total.shape, 0) % 8
    for step in (1, 2, 4):
        total = jnp.where((row & step) != 0, pltpu.roll(total, FILT - step, axis=1), total)
    return total.reshape(groups, 8, LANES).sum(axis=1)


def sums_kernel(key_ref, value_ref, query_ref, cot_ref, before_ref, sums_ref, head_ref):
    blocks = key_ref.shape[0] // FILT
    sums = []
    for tile in range(key_ref.shape[1] // LANES):
        lanes = slice(tile * LANES, (tile + 1) * LANES)
        products = rounded_product(key_ref[:, lanes], value_ref[:, lanes])
        grads = rounded_product(cot_ref[:, lanes], query_ref[:, lanes])
        head_ref[:, lanes] = grads[:FILT]
        ours = packed_halves([grads[b * FILT : (b + 1) * FILT] for b in range(blocks)])
        theirs = packed_halves(
            [before_ref[:, lanes]] + [products[b * FILT : (b + 1) * FILT] for b in range(blocks)]
        )
        pairs = range(0, blocks, 2)
        for half in range(2):
            left = jnp.concatenate([ours(half, b, b + 1) for b in pairs], axis=1)
            earlier = jnp.concatenate([theirs(half, b, b + 1) for b in pairs], axis=1)
            own = jnp.concatenate([theirs(half, b + 1, b + 2) for b in pairs], axis=1)
            sums.append(diagonal_sums(left, jnp.concatenate([earlier, own], axis=0), HALF))
    sums_ref[...] = jnp.concatenate(sums, axis=0)


def ordered_kernel(sums_ref, before_ref, head_ref, out_ref, total_ref):
    total_ref[...] = sums_ref[...]

    @pl.when(is_late())
    def _():
        groups = LANES // GROUP
        lane_group = (iota((FILT, 2 * LANES), 1) % LANES) // GROUP
        zero = jnp.zeros((FILT, 2 * LANES), BF16)
        same = iota((FILT, FILT), 0) >= iota((FILT, FILT), 1)
        row = iota((2 * groups * 8, LANES), 0) % 8
        for tile in range(0, head_ref.shape[1] // LANES, 2):
            lanes = slice(tile * LANES, (tile + 2) * LANES)
            head, before = head_ref[:, lanes], before_ref[:, lanes]
            left = jnp.concatenate([jnp.where(lane_group == g, head, zero) for g in range(groups)], axis=0)
            first = iota((FILT, 2 * LANES), 1) < LANES
            right = jnp.concatenate([jnp.where(first, before, zero), jnp.where(first, zero, before)], axis=0)
            outer = lax.dot_general(left, right, NT, preferred_element_type=F32)
            total = jnp.zeros(row.shape, F32)
            for i in range(0, FILT, 8):
                parts = []
                for side in range(2):
                    for g in range(groups):
                        part = outer[g * FILT + i : g * FILT + i + 8, side * FILT : (side + 1) * FILT]
                        parts.append(jnp.where(same[i : i + 8], 0.0, part))
                part = jnp.concatenate(parts, axis=0)
                total = total + (pltpu.roll(part, FILT - i, axis=1) if i else part)
            for step in (1, 2, 4):
                total = jnp.where((row & step) != 0, pltpu.roll(total, FILT - step, axis=1), total)
            rows = slice(tile * groups, (tile + 2) * groups)
            total_ref[rows] = total_ref[rows] + total.reshape(2 * groups, 8, LANES).sum(axis=1)

    out_ref[...] = jnp.dot(total_ref[...].astype(BF16), flip_table(), preferred_element_type=F32)


def message_kernel(sums_ref, taps_ref, out_ref):
    half = sums_ref.shape[0] // 2
    taps = taps_ref[...]
    halves = [
        jnp.concatenate([sums_ref[h * half : (h + 1) * half], taps], axis=0).astype(BF16) for h in range(2)
    ]
    for peer in range(out_ref.shape[0]):
        out_ref[peer] = halves[peer % 2]


def landing(ctx, fsdp):
    column, half = ctx // 2, ctx % 2
    x, hi = fsdp // SIDE, fsdp % SIDE
    place = (x + 2) % SIDE * SIDE + LANDING[column % SIDE][hi]
    return place * 2 + half, column


def by_column(column, values):
    out = values[1]
    for q in (0, 3):
        out = jnp.where(column % SIDE == q, values[q], out)
    return out


def landed_piece(ctx, column):
    low = ctx // 2 % SIDE
    hi = jnp.int32(0)
    for z in range(SIDE):
        hi = jnp.where(low == z, by_column(column, [jnp.int32(LANDING[q].index(z)) for q in range(SIDE)]), hi)
    return (ctx // 8 + 2) % SIDE * SIDE + hi


def reduce_kernel(recv_ref, filt_ref, flipped_ref, home_ref):
    peers = recv_ref.shape[0]
    half = GROUP
    own, column = lax.axis_index("ctx"), lax.axis_index("fsdp")
    total = jnp.zeros((half, LANES), F32)
    landed = []
    for peer in range(peers):
        message = recv_ref[peer].astype(F32)
        total = total + message[:half]
        landed.append(message[half:])
    eye = (iota((2 * half, LANES), 0) == iota((2 * half, LANES), 1)).astype(BF16)
    turned = []
    for h in range(2):
        pieces = []
        for piece in range(peers // 2):
            x, hi = piece // SIDE, piece % SIDE
            places = [(x + 2) % SIDE * SIDE + LANDING[q][hi] for q in range(SIDE)]
            pieces.append(by_column(column, [landed[2 * place + h] for place in places]))
        pieces = jnp.concatenate(pieces, axis=0).astype(BF16)
        turned.append(lax.dot_general(eye, pieces, NT, preferred_element_type=F32))
    high = jnp.concatenate([t[:half] for t in turned], axis=0)
    filt_ref[...] = high
    flipped_ref[...] = jnp.dot(high.astype(BF16), flip_table(), preferred_element_type=F32)
    decayed = [t[:half] + t[half:] for t in turned]
    own_decayed = jnp.where(own % 2 == 0, decayed[0], decayed[1])
    lane = iota((half, LANES), 1)
    rate = jnp.sum(own_decayed * total * lane.astype(F32), axis=1, keepdims=True)
    tap_count = FILT * 2 // peers
    moved = pltpu.roll(total, (FILT - tap_count * landed_piece(own, column)) % FILT, axis=1)
    home_ref[...] = jnp.where(lane < tap_count, moved, rate)


def circulants(rows):
    return jnp.concatenate(
        [
            pltpu.roll(jnp.broadcast_to(rows[g : g + 1], (FILT, FILT)), 0, axis=1, stride=1, stride_axis=0)
            for g in range(rows.shape[0])
        ],
        axis=0,
    )


def banded_pair(rows, first, second):
    whole = circulants(rows)
    zero = jnp.zeros_like(whole)
    return jnp.concatenate([jnp.where(first, whole, zero), jnp.where(second, whole, zero)], axis=1).astype(BF16)


def apply_filters(band, padded, blocks):
    groups, step = LANES // GROUP, 32
    right = jnp.concatenate([padded[b * FILT : (b + 2) * FILT] for b in range(blocks)], axis=1)
    lane_group = iota((step, LANES), 1) // GROUP
    parts = [[] for _ in range(blocks)]
    for first in range(0, FILT, step):
        left = jnp.concatenate([band[g * FILT + first : g * FILT + first + step] for g in range(groups)], axis=0)
        wide = jnp.dot(left, right, preferred_element_type=F32)
        for b in range(blocks):
            lanes = slice(b * LANES, (b + 1) * LANES)
            kept = wide[:step, lanes]
            for g in range(1, groups):
                kept = jnp.where(lane_group == g, wide[g * step : (g + 1) * step, lanes], kept)
            parts[b].append(kept)
    return [jnp.concatenate(p, axis=0) for p in parts]


def outputs_kernel(
    key_ref, value_ref, query_ref, cot_ref, early_ref, late_ref, after_ref, filt_ref, flipped_ref, *rest
):
    places, buffers, sems = rest[:4], rest[4:8], rest[8]
    blocks = key_ref.shape[0] // FILT
    groups = LANES // GROUP
    shape = (groups * FILT, FILT)
    row, col = iota(shape, 0) % FILT, iota(shape, 1)
    copies = []

    def send(index, tile):
        lanes = pl.ds(tile * LANES, LANES)
        copy = pltpu.make_async_copy(
            buffers[index].at[:, lanes], places[index].at[:, lanes], sems.at[len(copies)]
        )
        copy.start()
        copies.append(copy)

    for tile in range(key_ref.shape[1] // LANES):
        lanes = slice(tile * LANES, (tile + 1) * LANES)
        own = slice(tile * groups, (tile + 1) * groups)
        key, value = key_ref[:, lanes].astype(F32), value_ref[:, lanes].astype(F32)
        query, cot = query_ref[:, lanes].astype(F32), cot_ref[:, lanes].astype(F32)
        before = jnp.where(is_late(), late_ref[:, lanes], early_ref[:, lanes])
        products = jnp.concatenate([before, (key * value).astype(BF16)], axis=0)
        forward = banded_pair(flipped_ref[own], row < col, row >= col)
        for b, mixed in enumerate(apply_filters(forward, products, blocks)):
            rows = slice(b * FILT, (b + 1) * FILT)
            buffers[0][rows, lanes] = (query[rows] * mixed).astype(BF16)
            buffers[1][rows, lanes] = (cot[rows] * mixed).astype(BF16)
        send(0, tile)
        send(1, tile)
        grads = jnp.concatenate([(cot * query).astype(BF16), after_ref[:, lanes]], axis=0)
        backward = banded_pair(filt_ref[own], row <= col, row > col)
        for b, back in enumerate(apply_filters(backward, grads, blocks)):
            rows = slice(b * FILT, (b + 1) * FILT)
            buffers[2][rows, lanes] = (back * value[rows]).astype(BF16)
            buffers[3][rows, lanes] = (back * key[rows]).astype(BF16)
        send(2, tile)
        send(3, tile)
    for copy in copies:
        copy.wait()


def finish_kernel(home_ref, rate_ref, grad_filter_ref, grad_rate_ref, *, scale):
    tap_count, group_count = grad_filter_ref.shape
    turned = home_ref[...].T
    first_tap = lax.axis_index("fsdp") * tap_count
    taps = (first_tap + iota((tap_count, group_count), 0)).astype(F32)
    rates = jnp.exp(rate_ref[...])
    grad_filter_ref[...] = turned[:tap_count, :group_count] * jnp.exp(-rates * taps) * scale
    grad_rate_ref[...] = turned[tap_count : tap_count + 1, :group_count] * (-rates) * scale


def in_hbm(value):
    return pltpu.with_memory_space_constraint(value, pltpu.HBM)


def params(mib=24):
    return pltpu.CompilerParams(vmem_limit_bytes=mib * MIB)


def cost(us):
    return pl.CostEstimate(flops=int(us * 1e9), bytes_accessed=int(us * 3_000_000), transcendentals=0)


def moved_pieces(value, back):
    ctx, fsdp = lax.axis_size("ctx"), lax.axis_size("fsdp")
    pairs = []
    for c in range(ctx):
        for f in range(fsdp):
            there, column = landing(c, f)
            pairs.append((c * fsdp + f, there * fsdp + column))
    return lax.ppermute(value, ("ctx", "fsdp"), [(b, a) for a, b in pairs] if back else pairs)


def passed_along(value, by, chosen=lambda column: True):
    ctx, fsdp = lax.axis_size("ctx"), lax.axis_size("fsdp")
    pairs = [
        (c * fsdp + f, (c + by) * fsdp + f)
        for c in range(ctx) for f in range(fsdp) if 0 <= c + by < ctx and chosen(f)
    ]
    return lax.ppermute(value, ("ctx", "fsdp"), pairs)


def per_device(query, key_in, value_in, cotangent, filter_weight, log_rate):
    tokens, channels = query.shape
    peers = lax.axis_size("ctx")
    groups = channels // GROUP
    scale = 1.0 / math.sqrt(tokens * peers * GROUP)
    rate_row = log_rate.reshape(1, -1)
    sds = jax.ShapeDtypeStruct
    tap_count, tap_groups = filter_weight.shape

    edge = (FILT, channels)
    anywhere = pl.BlockSpec(memory_space=pl.ANY)
    tail, taps = pl.pallas_call(
        front_kernel,
        in_specs=[anywhere] * 6,
        out_shape=[sds(edge, BF16)] + [sds((tap_count, LANES), F32)],
        scratch_shapes=[pltpu.VMEM(filter_weight.shape, F32), pltpu.VMEM(rate_row.shape, F32)]
        + [pltpu.VMEM(edge, BF16)] * 2
        + [pltpu.SemaphoreType.DMA((4,))],
        compiler_params=params(),
    )(*(in_hbm(x) for x in (key_in, value_in, query, cotangent, filter_weight, rate_row)))
    taps_here = moved_pieces(taps, False)
    early = passed_along(tail, 1, lambda f: f % SIDE == 0)
    late_tail = pl.pallas_call(
        tail_kernel, out_shape=sds(edge, BF16), compiler_params=params()
    )(key_in, value_in)
    late = passed_along(late_tail, 1, lambda f: f % SIDE != 0)

    sums, head = pl.pallas_call(
        sums_kernel,
        out_shape=[sds((groups, LANES), F32), sds(edge, BF16)],
        cost_estimate=cost(3),
        compiler_params=params(),
    )(key_in, value_in, query, cotangent, early)
    after = passed_along(head, -1)
    sums = pl.pallas_call(
        ordered_kernel,
        out_shape=sds((groups, LANES), F32),
        scratch_shapes=[pltpu.VMEM((groups, LANES), F32)],
        compiler_params=params(),
    )(sums, late, head)
    message = pl.pallas_call(
        message_kernel,
        out_shape=sds((peers, groups // 2 + tap_count, LANES), BF16),
        compiler_params=params(),
    )(sums, taps_here)
    received = lax.all_to_all(message, "ctx", 0, 0, tiled=True)
    filt, flipped, home = pl.pallas_call(
        reduce_kernel,
        out_shape=[sds((groups, LANES), F32), sds((groups, LANES), F32), sds((groups // 2, LANES), F32)],
        compiler_params=params(),
    )(received)
    home = moved_pieces(home, True)
    output, grad_query, grad_key, grad_value = pl.pallas_call(
        outputs_kernel,
        out_specs=[anywhere] * 4,
        out_shape=[sds((tokens, channels), BF16)] * 4,
        scratch_shapes=[pltpu.VMEM((tokens, channels), BF16)] * 4
        + [pltpu.SemaphoreType.DMA((4 * channels // LANES,))],
        compiler_params=params(),
    )(key_in, value_in, query, cotangent, early, late, after, filt, flipped)
    grad_filter, grad_rate = pl.pallas_call(
        lambda *refs: finish_kernel(*refs, scale=scale),
        out_shape=[sds(filter_weight.shape, F32), sds(rate_row.shape, F32)],
        compiler_params=params(),
    )(home, rate_row)
    return (output, grad_query, grad_key, grad_value, grad_filter, grad_rate.reshape(log_rate.shape))


def solution(mesh):
    specs = (P("ctx", "fsdp"),) * 4 + (P("fsdp", "ctx"), P("ctx"))
    return jax.shard_map(per_device, mesh=mesh, in_specs=specs, out_specs=specs, check_vma=False)
```

```python
import math

import jax
import jax.numpy as jnp
from jax import lax
from jax.experimental import pallas as pl
from jax.experimental.pallas import tpu as pltpu
from jax.sharding import PartitionSpec as P

FILT = 128
GROUP = 16
LANES = 128
F32 = jnp.float32
BF16 = jnp.bfloat16
MIB = 1024 * 1024
NT = (((1,), (1,)), ((), ()))


def iota(shape, dim):
    return lax.broadcasted_iota(jnp.int32, shape, dim)


def flip_table():
    return ((iota((FILT, FILT), 0) + iota((FILT, FILT), 1)) % FILT == 0).astype(BF16)


def rounded_product(a, b):
    return (a.astype(F32) * b.astype(F32)).astype(BF16)


def front_kernel(key, value, query, cot, weight, rate, tail_ref, taps_ref, *scratch):
    refs, sems = scratch[:-1], scratch[-1]
    tail = pl.ds(key.shape[0] - FILT, FILT)
    sources = [weight, rate, key.at[tail], value.at[tail]]
    copies = [pltpu.make_async_copy(s, d, sems.at[i]) for i, (s, d) in enumerate(zip(sources, refs))]
    for copy in copies[:2]:
        copy.start()

    @pl.when(jnp.logical_not(is_late()))
    def _():
        for copy in copies[2:]:
            copy.start()

    weight_ref, rate_ref = refs[:2]
    tap_count, group_count = weight.shape
    taps = (lax.axis_index("fsdp") * tap_count + iota((tap_count, group_count), 0)).astype(F32)
    taps_ref[...] = jnp.zeros_like(taps_ref)
    for copy in copies[:2]:
        copy.wait()
    decayed = weight_ref[...] * jnp.exp(-jnp.exp(rate_ref[...]) * taps)
    high = decayed.astype(BF16).astype(F32)
    taps_ref[:, :group_count] = high
    taps_ref[:, group_count : 2 * group_count] = decayed - high

    @pl.when(jnp.logical_not(is_late()))
    def _():
        for copy in copies[2:]:
            copy.wait()
        tail_ref[...] = rounded_product(refs[2][...], refs[3][...])


def tail_kernel(key_ref, value_ref, tail_ref):
    tail_ref[...] = rounded_product(key_ref[-FILT:], value_ref[-FILT:])


LANDING = ((1, 2, 3, 0), (0, 1, 2, 3), (0, 1, 2, 3), (2, 0, 1, 3))
SIDE = 4


def is_late():
    return lax.axis_index("fsdp") % SIDE != 0


HALF = LANES // 2


def packed_halves(blocks_list):
    low = iota((FILT, LANES), 1) < HALF
    turned = [pltpu.roll(x, HALF, axis=1) for x in blocks_list]

    def pair(half, i, j):
        first, second = (blocks_list[i], turned[j]) if half == 0 else (turned[i], blocks_list[j])
        return jnp.where(low, first, second)

    return pair


def diagonal_sums(left, right, period):
    step, groups = FILT // 2, period // GROUP
    lane_group = (iota((step, left.shape[1]), 1) % period) // GROUP
    zero = jnp.zeros((step, left.shape[1]), BF16)
    total = jnp.zeros((groups * 8, LANES), F32)
    for first in range(0, FILT, step):
        rows = left[first : first + step]
        stacked = jnp.concatenate([jnp.where(lane_group == g, rows, zero) for g in range(groups)], axis=0)
        outer = lax.dot_general(stacked, right, NT, preferred_element_type=F32)
        for i in range(first, first + step, 8):
            same = iota((8, FILT), 0) + i >= iota((8, FILT), 1)
            parts = []
            for g in range(groups):
                row = slice(g * step + i - first, g * step + i - first + 8)
                before = outer[row, :FILT]
                own = outer[row, FILT:] if right.shape[0] > FILT else jnp.zeros_like(before)
                parts.append(jnp.where(same, own, before))
            part = jnp.concatenate(parts, axis=0)
            total = total + (pltpu.roll(part, FILT - i, axis=1) if i else part)
    row = iota(total.shape, 0) % 8
    for step in (1, 2, 4):
        total = jnp.where((row & step) != 0, pltpu.roll(total, FILT - step, axis=1), total)
    return total.reshape(groups, 8, LANES).sum(axis=1)


def sums_kernel(key_ref, value_ref, query_ref, cot_ref, before_ref, sums_ref, head_ref):
    blocks = key_ref.shape[0] // FILT
    sums = []
    for tile in range(key_ref.shape[1] // LANES):
        lanes = slice(tile * LANES, (tile + 1) * LANES)
        products = rounded_product(key_ref[:, lanes], value_ref[:, lanes])
        grads = rounded_product(cot_ref[:, lanes], query_ref[:, lanes])
        head_ref[:, lanes] = grads[:FILT]
        ours = packed_halves([grads[b * FILT : (b + 1) * FILT] for b in range(blocks)])
        theirs = packed_halves(
            [before_ref[:, lanes]] + [products[b * FILT : (b + 1) * FILT] for b in range(blocks)]
        )
        pairs = range(0, blocks, 2)
        for half in range(2):
            left = jnp.concatenate([ours(half, b, b + 1) for b in pairs], axis=1)
            earlier = jnp.concatenate([theirs(half, b, b + 1) for b in pairs], axis=1)
            own = jnp.concatenate([theirs(half, b + 1, b + 2) for b in pairs], axis=1)
            sums.append(diagonal_sums(left, jnp.concatenate([earlier, own], axis=0), HALF))
    sums_ref[...] = jnp.concatenate(sums, axis=0)


def ordered_kernel(sums_ref, before_ref, head_ref, out_ref, total_ref):
    total_ref[...] = sums_ref[...]

    @pl.when(is_late())
    def _():
        groups = LANES // GROUP
        lane_group = (iota((FILT, 2 * LANES), 1) % LANES) // GROUP
        zero = jnp.zeros((FILT, 2 * LANES), BF16)
        same = iota((FILT, FILT), 0) >= iota((FILT, FILT), 1)
        row = iota((2 * groups * 8, LANES), 0) % 8
        for tile in range(0, head_ref.shape[1] // LANES, 2):
            lanes = slice(tile * LANES, (tile + 2) * LANES)
            head, before = head_ref[:, lanes], before_ref[:, lanes]
            left = jnp.concatenate([jnp.where(lane_group == g, head, zero) for g in range(groups)], axis=0)
            first = iota((FILT, 2 * LANES), 1) < LANES
            right = jnp.concatenate([jnp.where(first, before, zero), jnp.where(first, zero, before)], axis=0)
            outer = lax.dot_general(left, right, NT, preferred_element_type=F32)
            total = jnp.zeros(row.shape, F32)
            for i in range(0, FILT, 8):
                parts = []
                for side in range(2):
                    for g in range(groups):
                        part = outer[g * FILT + i : g * FILT + i + 8, side * FILT : (side + 1) * FILT]
                        parts.append(jnp.where(same[i : i + 8], 0.0, part))
                part = jnp.concatenate(parts, axis=0)
                total = total + (pltpu.roll(part, FILT - i, axis=1) if i else part)
            for step in (1, 2, 4):
                total = jnp.where((row & step) != 0, pltpu.roll(total, FILT - step, axis=1), total)
            rows = slice(tile * groups, (tile + 2) * groups)
            total_ref[rows] = total_ref[rows] + total.reshape(2 * groups, 8, LANES).sum(axis=1)

    out_ref[...] = jnp.dot(total_ref[...].astype(BF16), flip_table(), preferred_element_type=F32)


def message_kernel(sums_ref, taps_ref, out_ref):
    half = sums_ref.shape[0] // 2
    taps = taps_ref[...]
    halves = [
        jnp.concatenate([sums_ref[h * half : (h + 1) * half], taps], axis=0).astype(BF16) for h in range(2)
    ]
    for peer in range(out_ref.shape[0]):
        out_ref[peer] = halves[peer % 2]


def landing(ctx, fsdp):
    column, half = ctx // 2, ctx % 2
    x, hi = fsdp // SIDE, fsdp % SIDE
    place = (x + 2) % SIDE * SIDE + LANDING[column % SIDE][hi]
    return place * 2 + half, column


def by_column(column, values):
    out = values[1]
    for q in (0, 3):
        out = jnp.where(column % SIDE == q, values[q], out)
    return out


def landed_piece(ctx, column):
    low = ctx // 2 % SIDE
    hi = jnp.int32(0)
    for z in range(SIDE):
        hi = jnp.where(low == z, by_column(column, [jnp.int32(LANDING[q].index(z)) for q in range(SIDE)]), hi)
    return (ctx // 8 + 2) % SIDE * SIDE + hi


def reduce_kernel(recv_ref, filt_ref, flipped_ref, home_ref):
    peers = recv_ref.shape[0]
    half = GROUP
    own, column = lax.axis_index("ctx"), lax.axis_index("fsdp")
    total = jnp.zeros((half, LANES), F32)
    landed = []
    for peer in range(peers):
        message = recv_ref[peer].astype(F32)
        total = total + message[:half]
        landed.append(message[half:])
    eye = (iota((2 * half, LANES), 0) == iota((2 * half, LANES), 1)).astype(BF16)
    turned = []
    for h in range(2):
        pieces = []
        for piece in range(peers // 2):
            x, hi = piece // SIDE, piece % SIDE
            places = [(x + 2) % SIDE * SIDE + LANDING[q][hi] for q in range(SIDE)]
            pieces.append(by_column(column, [landed[2 * place + h] for place in places]))
        pieces = jnp.concatenate(pieces, axis=0).astype(BF16)
        turned.append(lax.dot_general(eye, pieces, NT, preferred_element_type=F32))
    high = jnp.concatenate([t[:half] for t in turned], axis=0)
    filt_ref[...] = high
    flipped_ref[...] = jnp.dot(high.astype(BF16), flip_table(), preferred_element_type=F32)
    decayed = [t[:half] + t[half:] for t in turned]
    own_decayed = jnp.where(own % 2 == 0, decayed[0], decayed[1])
    lane = iota((half, LANES), 1)
    rate = jnp.sum(own_decayed * total * lane.astype(F32), axis=1, keepdims=True)
    tap_count = FILT * 2 // peers
    moved = pltpu.roll(total, (FILT - tap_count * landed_piece(own, column)) % FILT, axis=1)
    home_ref[...] = jnp.where(lane < tap_count, moved, rate)


def circulants(rows):
    return jnp.concatenate(
        [
            pltpu.roll(jnp.broadcast_to(rows[g : g + 1], (FILT, FILT)), 0, axis=1, stride=1, stride_axis=0)
            for g in range(rows.shape[0])
        ],
        axis=0,
    )


def banded_pair(rows, first, second):
    whole = circulants(rows)
    zero = jnp.zeros_like(whole)
    return jnp.concatenate([jnp.where(first, whole, zero), jnp.where(second, whole, zero)], axis=1).astype(BF16)


def apply_filters(band, padded, blocks):
    groups, step = LANES // GROUP, 32
    right = jnp.concatenate([padded[b * FILT : (b + 2) * FILT] for b in range(blocks)], axis=1)
    lane_group = iota((step, LANES), 1) // GROUP
    parts = [[] for _ in range(blocks)]
    for first in range(0, FILT, step):
        left = jnp.concatenate([band[g * FILT + first : g * FILT + first + step] for g in range(groups)], axis=0)
        wide = jnp.dot(left, right, preferred_element_type=F32)
        for b in range(blocks):
            lanes = slice(b * LANES, (b + 1) * LANES)
            kept = wide[:step, lanes]
            for g in range(1, groups):
                kept = jnp.where(lane_group == g, wide[g * step : (g + 1) * step, lanes], kept)
            parts[b].append(kept)
    return [jnp.concatenate(p, axis=0) for p in parts]


def outputs_kernel(
    key_ref, value_ref, query_ref, cot_ref, early_ref, late_ref, after_ref, filt_ref, flipped_ref, *rest
):
    places, buffers, sems = rest[:4], rest[4:8], rest[8]
    blocks = key_ref.shape[0] // FILT
    groups = LANES // GROUP
    shape = (groups * FILT, FILT)
    row, col = iota(shape, 0) % FILT, iota(shape, 1)
    copies = []

    def send(index, tile):
        lanes = pl.ds(tile * LANES, LANES)
        copy = pltpu.make_async_copy(
            buffers[index].at[:, lanes], places[index].at[:, lanes], sems.at[len(copies)]
        )
        copy.start()
        copies.append(copy)

    for tile in range(key_ref.shape[1] // LANES):
        lanes = slice(tile * LANES, (tile + 1) * LANES)
        own = slice(tile * groups, (tile + 1) * groups)
        key, value = key_ref[:, lanes].astype(F32), value_ref[:, lanes].astype(F32)
        query, cot = query_ref[:, lanes].astype(F32), cot_ref[:, lanes].astype(F32)
        before = jnp.where(is_late(), late_ref[:, lanes], early_ref[:, lanes])
        products = jnp.concatenate([before, (key * value).astype(BF16)], axis=0)
        forward = banded_pair(flipped_ref[own], row < col, row >= col)
        for b, mixed in enumerate(apply_filters(forward, products, blocks)):
            rows = slice(b * FILT, (b + 1) * FILT)
            buffers[0][rows, lanes] = (query[rows] * mixed).astype(BF16)
            buffers[1][rows, lanes] = (cot[rows] * mixed).astype(BF16)
        send(0, tile)
        send(1, tile)
        grads = jnp.concatenate([(cot * query).astype(BF16), after_ref[:, lanes]], axis=0)
        backward = banded_pair(filt_ref[own], row <= col, row > col)
        for b, back in enumerate(apply_filters(backward, grads, blocks)):
            rows = slice(b * FILT, (b + 1) * FILT)
            buffers[2][rows, lanes] = (back * value[rows]).astype(BF16)
            buffers[3][rows, lanes] = (back * key[rows]).astype(BF16)
        send(2, tile)
        send(3, tile)
    for copy in copies:
        copy.wait()


def finish_kernel(home_ref, rate_ref, grad_filter_ref, grad_rate_ref, *, scale):
    tap_count, group_count = grad_filter_ref.shape
    turned = home_ref[...].T
    first_tap = lax.axis_index("fsdp") * tap_count
    taps = (first_tap + iota((tap_count, group_count), 0)).astype(F32)
    rates = jnp.exp(rate_ref[...])
    grad_filter_ref[...] = turned[:tap_count, :group_count] * jnp.exp(-rates * taps) * scale
    grad_rate_ref[...] = turned[tap_count : tap_count + 1, :group_count] * (-rates) * scale


def in_hbm(value):
    return pltpu.with_memory_space_constraint(value, pltpu.HBM)


def params(mib=24):
    return pltpu.CompilerParams(vmem_limit_bytes=mib * MIB)


def cost(us):
    return pl.CostEstimate(flops=int(us * 1e9), bytes_accessed=int(us * 3_000_000), transcendentals=0)


def moved_pieces(value, back):
    ctx, fsdp = lax.axis_size("ctx"), lax.axis_size("fsdp")
    pairs = []
    for c in range(ctx):
        for f in range(fsdp):
            there, column = landing(c, f)
            pairs.append((c * fsdp + f, there * fsdp + column))
    return lax.ppermute(value, ("ctx", "fsdp"), [(b, a) for a, b in pairs] if back else pairs)


def passed_along(value, by, chosen=lambda column: True):
    ctx, fsdp = lax.axis_size("ctx"), lax.axis_size("fsdp")
    pairs = [
        (c * fsdp + f, (c + by) * fsdp + f)
        for c in range(ctx) for f in range(fsdp) if 0 <= c + by < ctx and chosen(f)
    ]
    return lax.ppermute(value, ("ctx", "fsdp"), pairs)


def per_device(query, key_in, value_in, cotangent, filter_weight, log_rate):
    tokens, channels = query.shape
    peers = lax.axis_size("ctx")
    groups = channels // GROUP
    scale = 1.0 / math.sqrt(tokens * peers * GROUP)
    rate_row = log_rate.reshape(1, -1)
    sds = jax.ShapeDtypeStruct
    tap_count, tap_groups = filter_weight.shape

    edge = (FILT, channels)
    anywhere = pl.BlockSpec(memory_space=pl.ANY)
    tail, taps = pl.pallas_call(
        front_kernel,
        in_specs=[anywhere] * 6,
        out_shape=[sds(edge, BF16)] + [sds((tap_count, LANES), F32)],
        scratch_shapes=[pltpu.VMEM(filter_weight.shape, F32), pltpu.VMEM(rate_row.shape, F32)]
        + [pltpu.VMEM(edge, BF16)] * 2
        + [pltpu.SemaphoreType.DMA((4,))],
        compiler_params=params(),
    )(*(in_hbm(x) for x in (key_in, value_in, query, cotangent, filter_weight, rate_row)))
    taps_here = moved_pieces(taps, False)
    early = passed_along(tail, 1, lambda f: f % SIDE == 0)
    late_tail = pl.pallas_call(
        tail_kernel, out_shape=sds(edge, BF16), compiler_params=params()
    )(key_in, value_in)
    late = passed_along(late_tail, 1, lambda f: f % SIDE != 0)

    sums, head = pl.pallas_call(
        sums_kernel,
        out_shape=[sds((groups, LANES), F32), sds(edge, BF16)],
        cost_estimate=cost(3),
        compiler_params=params(),
    )(key_in, value_in, query, cotangent, early)
    after = passed_along(head, -1)
    sums = pl.pallas_call(
        ordered_kernel,
        out_shape=sds((groups, LANES), F32),
        scratch_shapes=[pltpu.VMEM((groups, LANES), F32)],
        compiler_params=params(),
    )(sums, late, head)
    message = pl.pallas_call(
        message_kernel,
        out_shape=sds((peers, groups // 2 + tap_count, LANES), BF16),
        compiler_params=params(),
    )(sums, taps_here)
    received = lax.all_to_all(message, "ctx", 0, 0, tiled=True)
    filt, flipped, home = pl.pallas_call(
        reduce_kernel,
        out_shape=[sds((groups, LANES), F32), sds((groups, LANES), F32), sds((groups // 2, LANES), F32)],
        compiler_params=params(),
    )(received)
    home = moved_pieces(home, True)
    output, grad_query, grad_key, grad_value = pl.pallas_call(
        outputs_kernel,
        out_specs=[anywhere] * 4,
        out_shape=[sds((tokens, channels), BF16)] * 4,
        scratch_shapes=[pltpu.VMEM((tokens, channels), BF16)] * 4
        + [pltpu.SemaphoreType.DMA((4 * channels // LANES,))],
        compiler_params=params(),
    )(key_in, value_in, query, cotangent, early, late, after, filt, flipped)
    grad_filter, grad_rate = pl.pallas_call(
        lambda *refs: finish_kernel(*refs, scale=scale),
        out_shape=[sds(filter_weight.shape, F32), sds(rate_row.shape, F32)],
        compiler_params=params(),
    )(home, rate_row)
    return (output, grad_query, grad_key, grad_value, grad_filter, grad_rate.reshape(log_rate.shape))


def solution(mesh):
    specs = (P("ctx", "fsdp"),) * 4 + (P("fsdp", "ctx"), P("ctx"))
    return jax.shard_map(per_device, mesh=mesh, in_specs=specs, out_specs=specs, check_vma=False)
```
